32 devices in a mesh: group: 4 (over x, core), dp: 2 (over y), tensor: 4 (over z).
Axes of the slice: x: 2, y: 2, z: 4, core: 2. Of those that a mesh axis runs over, the one named last changes fastest.
Arguments:
- activations: bfloat16 [6144, 5120], P(('group', 'dp'), 'tensor'), may hold values from -6 to 6
- norm_gain: float32 [5120], replicated, may hold values from 0.5 to 1.5
- master_weight: float32 [5120, 4, 3, 128], P(('group', 'dp'), 'tensor'), may hold values from -0.078125 to 0.078125
- grad: bfloat16 [5120, 4, 3, 128], P(('group', 'dp'), 'tensor'), may hold values from -12 to 12
- moment: float32 [5120, 4, 3, 128], P(('group', 'dp'), 'tensor'), may hold values from -0.0048828125 to 0.0048828125
- variance: float32 [5120, 4, 3, 128], P(('group', 'dp'), 'tensor'), may hold values from 6.357829e-09 to 2.5431316e-07
- query_gain: float32 [8, 128], P('tensor'), may hold values from 1 to 2.5
- key_gain: float32 [2, 128], replicated, may hold values from 1 to 2.5
- prompt_len: int32 [8], P(('group', 'dp')), may hold values from 192 to 768, as said below
Outputs:
- attended: bfloat16 [6144, 1024], P(('group', 'dp'), 'tensor')
The draws below stay inside these ranges and needn't reach their ends.
Inputs may be any that keep to these rules, and one draw needn't show every extreme that they name: `prompt_len`: some sequence is full.
All inputs are finite; a program needn't handle non-finite values.
Results may differ from the reference program's by a relative error of at most 0.012.
The reference program's roundings to bfloat16 on the way (of `updated`, `normed` and `weights`) count: a program that leaves them out, or rounds other values in their place, can miss the bound.
Values may be sent and summed in bfloat16 or wider, within the bound.
A program may use at most 64 MiB of HBM per device.

```python
import math
import jax
import jax.numpy as jnp
from jax import lax

D = 5120
HD = 128
HEAD_DEV = 2
SEQ = 768
HEADS = 8
KV_HEADS = 2
SEQS = 8
TOKENS = 6144


def draw_grad(key, part):
    key = jax.random.fold_in(key, 11)
    shape = (D, 2 * KV_HEADS, HEAD_DEV + 1, HD)
    rows = jnp.arange(D, dtype=jnp.float32) / (D - 1)
    ramp = (1.0 + 2.0 * rows)[:, None, None, None]
    slab_key = jax.random.fold_in(key, 5)
    block_key = jax.random.fold_in(key, 7)
    slab_factor = jnp.exp(jax.random.uniform(slab_key, (1, 2 * KV_HEADS, 1, 1), jnp.float32, -1.5, 1.5))
    block_table = jnp.exp(jax.random.uniform(block_key, (32,), jnp.float32, -1.5, 1.5))
    block_index = jnp.arange(D, dtype=jnp.int32) * 32 // D
    block_factor = jnp.take(block_table, block_index)[:, None, None, None]
    base = jnp.clip(jax.random.normal(key, shape, jnp.float32), -4.0, 4.0)
    values = 0.25 * base * ramp * slab_factor * block_factor
    return jnp.clip(values, -12.0, 12.0).astype(jnp.bfloat16)


def draw_prompt_len(key, part):
    key = jax.random.fold_in(key, 23)
    lengths = jax.random.randint(key, (SEQS,), SEQ // 4, SEQ + 1, dtype=jnp.int32)
    return lengths.at[0].set(SEQ)


def levels(stream_key, dims, pieces, smallest, top_value):
    level = 1.0
    for dim, parts in pieces:
        heights = jax.random.uniform(jax.random.fold_in(jax.random.fold_in(stream_key, 6), dim), (parts,), jnp.float32, smallest / len(pieces), top_value / len(pieces))
        level = level * jnp.repeat(jnp.exp(heights), dims[dim] // parts).reshape((-1,) + (1,) * (len(dims) - 1 - dim))
    return level


def normal_values(key, extent, scale, limit, cuts=(), kind=jnp.bfloat16):
    result = scale * jax.random.normal(key, extent, jnp.float32)
    if cuts:
        result = result * levels(key, extent, cuts, -0.22, 0.18)
    return jnp.clip(result, -limit, limit).astype(kind)


def setup_inputs(seed: int = 0) -> dict:
    seeds = jax.random.split(jax.random.key(seed), 10)
    activations = normal_values(seeds[0], (TOKENS, D), 1.0, 6.0, ((0, 8), (1, 4)))
    norm_gain = jnp.clip(jax.random.uniform(seeds[1], (D,), jnp.float32, 0.5, 1.5), 0.5, 1.5)
    master_weight = normal_values(seeds[2], (D, 2 * KV_HEADS, HEAD_DEV + 1, HD), D ** -0.5, 0.078125, ((0, 8), (1, 4)), jnp.float32)
    grad = draw_grad(jax.random.fold_in(seeds[9], 71), 0)
    moment = normal_values(seeds[4], (D, 2 * KV_HEADS, HEAD_DEV + 1, HD), ((D * 2 * KV_HEADS * (HEAD_DEV + 1) * HD) ** -0.5), 0.0048828125, ((0, 8), (1, 4)), jnp.float32)
    variance = jnp.clip(jnp.exp(math.log(2.5431316430513107e-07) - 3.6888795 * jax.random.uniform(seeds[5], (D, 2 * KV_HEADS, HEAD_DEV + 1, HD), jnp.float32) ** levels(seeds[5], (D, 2 * KV_HEADS, HEAD_DEV + 1, HD), ((0, 8), (1, 4)), -0.2, 0.2)), 6.357828929992593e-09, 2.5431316430513107e-07)
    query_gain = jnp.clip(1.0 + 1.5 * jax.random.uniform(seeds[6], (HEADS, HD), jnp.float32) ** levels(seeds[6], (HEADS, HD), ((0, 4),), -0.2, 0.2), 1.0, 2.5)
    key_gain = jnp.clip(jax.random.uniform(seeds[7], (KV_HEADS, HD), jnp.float32, 1.0, 2.5), 1.0, 2.5)
    prompt_len = draw_prompt_len(jax.random.fold_in(seeds[9], 71), 0)
    return dict(activations=activations, norm_gain=norm_gain, master_weight=master_weight, grad=grad, moment=moment, variance=variance, query_gain=query_gain, key_gain=key_gain, prompt_len=prompt_len)


STEP_SCALE = 0.5
BETA_ONE = 0.9
BETA_TWO = 0.95
ROPE_BASE = 500000.0

def rope_tables(length, head_size):
    positions = jnp.arange(length, dtype=jnp.float32)
    exponent = jnp.arange(head_size // 2, dtype=jnp.float32) * 2.0 / head_size
    inverse = jnp.power(ROPE_BASE, -exponent)
    angles = positions[:, None] * inverse[None, :]
    return (jnp.cos(angles), jnp.sin(angles))

def rotate(inputs, cosine, sine):
    midpoint = inputs.shape[-1] // 2
    front_half = inputs[..., :midpoint]
    back_half = inputs[..., midpoint:]
    return jnp.concatenate([front_half * cosine - back_half * sine, back_half * cosine + front_half * sine], axis=-1)

def rms_scaled(inputs, gains):
    return inputs * lax.rsqrt(lax.optimization_barrier(jnp.mean(inputs * inputs, axis=-1, keepdims=True)) + 1e-06) * gains

def attend(query_proj, key_proj, value_proj, query_gain, key_gain, length):
    length_seq = query_proj.shape[0]
    head_count = query_proj.shape[1]
    pair_count = key_proj.shape[1]
    head_size = query_proj.shape[-1]
    cosine, sine = rope_tables(length_seq, head_size)
    cosine = cosine[:, None, :]
    sine = sine[:, None, :]
    queries = rms_scaled(query_proj, query_gain)
    keys_raw = rms_scaled(key_proj, key_gain)
    queries = (rotate(queries, cosine, sine) * head_size ** (-0.5)).astype(jnp.bfloat16)
    key_rot = rotate(keys_raw, cosine, sine).astype(jnp.bfloat16)
    value_rows = value_proj.astype(jnp.bfloat16)
    grouped = queries.reshape(length_seq, pair_count, head_count // pair_count, head_size)
    scores = jnp.einsum('qgje,kge->gjqk', grouped.astype(jnp.float32), key_rot.astype(jnp.float32))
    row_pos = jnp.arange(length_seq, dtype=jnp.int32)[:, None]
    col_pos = jnp.arange(length_seq, dtype=jnp.int32)[None, :]
    allowed = (col_pos <= row_pos) & (col_pos < length)
    scores = jnp.where(allowed[None, None], scores, -1e+30)
    highest = lax.optimization_barrier(jnp.max(scores, axis=-1, keepdims=True))
    weights = jnp.exp(scores - highest)
    weights = (weights / lax.optimization_barrier(jnp.sum(weights, axis=-1, keepdims=True))).astype(jnp.bfloat16)
    output = jnp.einsum('gjqk,kge->qgje', weights.astype(jnp.float32), value_rows.astype(jnp.float32))
    return output.astype(jnp.bfloat16).reshape(length_seq, -1)

def reference(activations, norm_gain, master_weight, grad, moment, variance, query_gain, key_gain, prompt_len):
    grad_full = grad.astype(jnp.float32)
    sumsq = jnp.sum(grad_full * grad_full)
    clip_factor = 1.0 / jnp.sqrt(sumsq + 1e-12)
    clipped = grad_full * clip_factor
    moment_new = BETA_ONE * moment + (1.0 - BETA_ONE) * clipped
    variance_new = BETA_TWO * variance + (1.0 - BETA_TWO) * clipped * clipped
    step_size = STEP_SCALE * D ** (-0.5)
    updated = (master_weight - step_size * moment_new / (jnp.sqrt(variance_new) + 1e-08)).astype(jnp.bfloat16)
    width_all = updated.shape[0]
    slab_count = updated.shape[1]
    head_dev = updated.shape[2] - 1
    head_size = updated.shape[3]
    query_weight = updated[:, :, :head_dev].reshape(width_all, slab_count * head_dev * head_size)
    pair_weight = updated[:, :, head_dev].reshape(width_all, slab_count * head_size)
    sequences = activations.reshape(-1, SEQ, width_all)

    def one_sequence(inputs):
        rows_in, length = inputs
        widened = rows_in.astype(jnp.float32)
        row_scale = lax.rsqrt(lax.optimization_barrier(jnp.mean(widened * widened, axis=-1, keepdims=True)) + 1e-06)
        normed = (widened * row_scale * norm_gain).astype(jnp.bfloat16)
        query_proj = jnp.dot(normed, query_weight, preferred_element_type=jnp.float32)
        query_proj = query_proj.reshape(SEQ, slab_count * head_dev, head_size)
        pair_proj = jnp.dot(normed, pair_weight, preferred_element_type=jnp.float32)
        pair_proj = pair_proj.reshape(SEQ, slab_count // 2, 2, head_size)
        return attend(query_proj, pair_proj[:, :, 0], pair_proj[:, :, 1], query_gain, key_gain, length)
    outputs = lax.map(one_sequence, (sequences, prompt_len))
    return outputs.reshape(-1, slab_count * head_dev * head_size)
```

```python
import functools

import jax
import jax.numpy as jnp
import numpy as np
from jax import lax
from jax.experimental import pallas as pl
from jax.experimental.pallas import tpu as pltpu
from jax.sharding import PartitionSpec as P

STEP_SCALE = 0.5
BETA_ONE = 0.9
BETA_TWO = 0.95
ROPE_BASE = 500000.0
MESH = pl.DeviceIdType.MESH
BF16 = jnp.bfloat16
F32 = jnp.float32


def rope_tables(length, head_size):
    positions = np.arange(length, dtype=np.float32)
    exponent = np.arange(head_size // 2, dtype=np.float32) * np.float32(2.0) / np.float32(head_size)
    inverse = np.power(np.float32(ROPE_BASE), -exponent).astype(np.float32)
    angles = (positions[:, None] * inverse[None, :]).astype(np.float32)
    cosine, sine = np.cos(angles), np.sin(angles)
    return (
        np.concatenate([cosine, cosine], axis=1).astype(np.float32),
        np.concatenate([-sine, sine], axis=1).astype(np.float32),
    )


def kernel(
    sizes,
    act_hbm, gain_ref, master_hbm, grad_hbm, moment_hbm, variance_hbm, query_gain_ref, key_gain_ref,
    cos_ref, sin_ref, len_ref,
    out_ref,
    act, normed, master, grad, moment, variance, q_own, kv_own, weights, parts, up, down, final, queries, keys, values,
    plane_sum, line_sum, row_sum,
    in_sem, plane_send, plane_recv, line_send, line_recv, row_send, row_recv,
    hub_send, w_recv, w_send, up_send, up_recv, down_send, down_recv,
):
    group_n, dp_n, tensor_n, width = sizes
    plane_n = group_n * dp_n
    chip_n = group_n // 2
    hubs = plane_n // tensor_n
    length, feat = act.shape
    slab_rows = grad.shape[1]
    blocks = weights.shape[0]
    head = 128
    chunk = 256 if length % 256 == 0 else length
    chunks = length // chunk

    g = lax.axis_index("group")
    d = lax.axis_index("dp")
    z = lax.axis_index("tensor")
    me = g * dp_n + d
    x, core = g // 2, g % 2

    def plane_peer(i):
        p = (me + i) % plane_n
        return p, (p // dp_n, p % dp_n, z)

    def line_peer(i):
        t = (z + i) % tensor_n
        return t, (g, d, t)

    loads = [
        pltpu.make_async_copy(src, dst, in_sem.at[i])
        for i, (src, dst) in enumerate(
            [(grad_hbm, grad), (act_hbm, act), (moment_hbm, moment), (variance_hbm, variance), (master_hbm, master)]
        )
    ]
    for load in loads:
        load.start()

    barrier = pltpu.get_barrier_semaphore()
    for i in range(1, plane_n):
        pl.semaphore_signal(barrier, inc=1, device_id=plane_peer(i)[1], device_id_type=MESH)
    for i in range(1, tensor_n):
        pl.semaphore_signal(barrier, inc=1, device_id=line_peer(i)[1], device_id_type=MESH)

    loads[0].wait()
    tile = jnp.zeros((8, head), F32)
    for s in range(3):
        piece = grad[s].astype(F32)
        tile += jnp.sum((piece * piece).reshape(slab_rows // 8, 8, head), axis=0)
    plane_sum[me] = tile
    pl.semaphore_wait(barrier, plane_n + tensor_n - 2)

    def exchange(buf, slot, dev, ssem, rsem):
        return pltpu.make_async_remote_copy(
            src_ref=buf.at[slot], dst_ref=buf.at[slot], send_sem=ssem, recv_sem=rsem.at[slot],
            device_id=dev, device_id_type=MESH,
        )

    for i in range(1, plane_n):
        exchange(plane_sum, me, plane_peer(i)[1], plane_send.at[i], plane_recv).start()

    loads[1].wait()
    for c in range(chunks):
        rows = pl.ds(c * chunk, chunk)
        wide = act[rows, :].astype(F32)
        column = jnp.sum(wide * wide, axis=1, keepdims=True)
        row_sum[z, :, rows] = jnp.broadcast_to(column, (chunk, head)).T[:8]
    for i in range(1, tensor_n):
        exchange(row_sum, z, line_peer(i)[1], row_send.at[i], row_recv).start()

    total = plane_sum[me]
    for i in range(1, plane_n):
        p, dev = plane_peer(i)
        exchange(plane_sum, p, dev, plane_send.at[i], plane_recv).wait_recv()
        total += plane_sum[p]
    line_sum[z] = total
    for i in range(1, tensor_n):
        exchange(line_sum, z, line_peer(i)[1], line_send.at[i], line_recv).start()
    for load in loads[2:]:
        load.wait()
    for i in range(1, tensor_n):
        t, dev = line_peer(i)
        exchange(line_sum, t, dev, line_send.at[i], line_recv).wait_recv()
        total += line_sum[t]
    sumsq = jnp.sum(jnp.sum(total, axis=0, keepdims=True), axis=1, keepdims=True)
    clip = 1.0 / jnp.sqrt(sumsq + 1e-12)

    step_size = STEP_SCALE * width ** (-0.5)

    def updated(s):
        clipped = grad[s].astype(F32) * clip
        rows = pl.ds(s, slab_rows, stride=3)
        moment_new = BETA_ONE * moment[rows, :] + (1.0 - BETA_ONE) * clipped
        variance_new = BETA_TWO * variance[rows, :] + (1.0 - BETA_TWO) * clipped * clipped
        return (master[rows, :] - step_size * moment_new / (jnp.sqrt(variance_new) + 1e-08)).astype(BF16)

    def q_block(t):
        return 3 * (t // 2) + 2 * (t % 2)

    def kv_block(t):
        return 3 * (t // 2) + 1

    def w_slot(r, t, part):
        rows = pl.ds(pl.multiple_of(r * slab_rows, 16), slab_rows)
        if part == 0:
            return weights.at[q_block(t), rows, :]
        return weights.at[kv_block(t), rows, pl.ds(pl.multiple_of((t % 2) * head, head), head)]

    owner, my_r = me // hubs, me % hubs

    def to_hub(part):
        return pltpu.make_async_remote_copy(
            src_ref=(q_own, kv_own)[part], dst_ref=w_slot(my_r, z, part), send_sem=hub_send.at[part],
            recv_sem=w_recv.at[my_r, z, part], device_id=(g, d, owner), device_id_type=MESH,
        )

    def place(part):
        @pl.when(z == owner)
        def _():
            w_slot(my_r, z, part)[...] = (q_own, kv_own)[part][...]

        @pl.when(z != owner)
        def _():
            to_hub(part).start()

    q_own[:, :head] = updated(0)
    q_own[:, head:] = updated(1)
    place(0)
    kv_own[...] = updated(2)
    place(1)

    square = row_sum[z]
    for i in range(1, tensor_n):
        t, dev = line_peer(i)
        exchange(row_sum, t, dev, row_send.at[i], row_recv).wait_recv()
        square += row_sum[t]
    scale_row = lax.rsqrt(square[:1] * (1.0 / width) + 1e-06)
    for c in range(chunks):
        rows = pl.ds(c * chunk, chunk)
        scale = jnp.broadcast_to(scale_row[:, c * chunk : (c + 1) * chunk], (head, chunk)).T[:, :1]
        normed[rows, :] = (act[rows, :].astype(F32) * scale * gain_ref[z]).astype(BF16)

    def forward(r, t, part, slot, dev):
        return pltpu.make_async_remote_copy(
            src_ref=w_slot(r, t, part), dst_ref=w_slot(r, t, part), send_sem=w_send.at[r, t, part, slot],
            recv_sem=w_recv.at[r, t, part], device_id=dev, device_id_type=MESH,
        )

    def forwards(r, t, part, act_on):
        hub = z * hubs + r
        hub_g, hub_d = hub // dp_n, hub % dp_n
        same_core = core == hub_g % 2
        at_hub = hub == me

        @pl.when(at_hub)
        def _():
            for i in range(1, chip_n):
                act_on(forward(r, t, part, i - 1, (((x + i) % chip_n) * 2 + core, d, z)))

        @pl.when(jnp.logical_and(same_core, d == hub_d))
        def _():
            for i in range(1, dp_n):
                act_on(forward(r, t, part, chip_n - 2 + i, (g, (d + i) % dp_n, z)))

        @pl.when(same_core)
        def _():
            act_on(forward(r, t, part, chip_n + dp_n - 2, (x * 2 + 1 - core, d, z)))

    def start(copy):
        copy.start()

    def wait_send(copy):
        copy.wait_send()

    def chain(buf, b, c, dev_z, ssem, rsem):
        rows = pl.ds(pl.multiple_of(c * chunk, 16), chunk)
        return pltpu.make_async_remote_copy(
            src_ref=buf.at[b, rows, :], dst_ref=buf.at[b, rows, :], send_sem=ssem.at[b, c], recv_sem=rsem.at[b, c],
            device_id=(g, d, dev_z), device_id_type=MESH,
        )

    def chain_up(b, c):
        return chain(up, b, c, jnp.minimum(z + 1, tensor_n - 1), up_send, up_recv)

    def chain_down(b, c):
        return chain(down, b, c, jnp.maximum(z - 1, 0), down_send, down_recv)

    def span(b):
        pair, j = b // 3, b % 3
        return 2 * pair + j // 2, 2 * pair + (j + 1) // 2

    def multiply(b):
        low, high = span(b)

        @pl.loop(0, chunks)
        def _(c):
            rows = pl.ds(pl.multiple_of(c * chunk, 16), chunk)
            parts[b, rows, :] = jnp.dot(normed[rows, :], weights[b], preferred_element_type=F32)

            @pl.when(jnp.logical_and(z == 0, z < high))
            def _():
                up[b, rows, :] = parts[b, rows, :].astype(BF16)
                chain_up(b, c).start()

            @pl.when(jnp.logical_and(z == tensor_n - 1, z > low))
            def _():
                down[b, rows, :] = parts[b, rows, :].astype(BF16)
                chain_down(b, c).start()

    @pl.loop(0, 2 * tensor_n - 1)
    def _(k):
        distance = (k + 1) // 2
        t = z + distance * (2 * (k % 2) - 1)

        @pl.when(jnp.logical_and(t >= 0, t < tensor_n))
        def _():
            for r in range(hubs):
                for part in range(2):
                    @pl.when(jnp.logical_not(jnp.logical_and(z * hubs + r == me, t == z)))
                    def _():
                        forward(r, t, part, 0, (g, d, z)).wait_recv()

                    forwards(r, t, part, start)
            multiply(q_block(t))
            mate = t + 1 - 2 * (t % 2)
            offset = mate - z
            rank = jnp.where(offset > 0, 2 * offset - 1, -2 * offset)

            @pl.when(rank < k)
            def _():
                multiply(kv_block(t))

    mine = (q_block(z), kv_block(z))
    for slot in range(2):
        final[slot] = parts[mine[slot]]

    @pl.loop(0, blocks)
    def _(i):
        def hop(b, c, buf, copy, receives, sends):
            low, high = span(b)
            rows = pl.ds(pl.multiple_of(c * chunk, 16), chunk)

            @pl.when(receives)
            def _():
                copy(b, c).wait_recv()

                @pl.when(jnp.logical_and(low <= z, z <= high))
                def _():
                    slot = 1 - (b % 3 != 1).astype(jnp.int32)
                    final[slot, rows, :] += buf[b, rows, :].astype(F32)

                @pl.when(sends)
                def _():
                    buf[b, rows, :] = (parts[b, rows, :] + buf[b, rows, :].astype(F32)).astype(BF16)
                    copy(b, c).start()

        @pl.loop(0, chunks)
        def _(c):
            low, high = span(i)
            hop(i, c, up, chain_up, jnp.logical_and(z > 0, z <= high), z < high)
            j = blocks - 1 - i
            low, high = span(j)
            hop(j, c, down, chain_down, jnp.logical_and(z < tensor_n - 1, z >= low), z > low)

    def prepared(raw, gains, rows):
        scaled = raw * lax.rsqrt(jnp.mean(raw * raw, axis=1, keepdims=True) + 1e-06) * gains
        return scaled * cos_ref[rows, :] + pltpu.roll(scaled, head // 2, 1) * sin_ref[rows, :]

    key_gain = key_gain_ref[pl.ds(z // 2, 1), :]
    for c in range(chunks):
        rows = pl.ds(c * chunk, chunk)
        for j in range(2):
            raw = final[0, rows, j * head : (j + 1) * head]
            queries[j, rows, :] = (prepared(raw, query_gain_ref[j : j + 1, :], rows) * head ** (-0.5)).astype(BF16)
        keys[rows, :] = prepared(final[1, rows, :head], key_gain, rows).astype(BF16)
        values[rows, :] = final[1, rows, head:].astype(BF16)
    live = len_ref[0]
    for c in range(chunks):
        rows = pl.ds(c * chunk, chunk)
        seen = (c + 1) * chunk
        row_pos = lax.broadcasted_iota(jnp.int32, (chunk, seen), 0) + c * chunk
        col_pos = lax.broadcasted_iota(jnp.int32, (chunk, seen), 1)
        allowed = jnp.logical_and(col_pos <= row_pos, col_pos < live)
        for j in range(2):
            scores = lax.dot_general(
                queries[j, rows, :], keys[:seen, :], (((1,), (1,)), ((), ())), preferred_element_type=F32
            )
            scores = jnp.where(allowed, scores, -1e30)
            exps = jnp.exp(scores - jnp.max(scores, axis=1, keepdims=True))
            probs = (exps / jnp.sum(exps, axis=1, keepdims=True)).astype(BF16)
            out_ref[rows, j * head : (j + 1) * head] = jnp.dot(
                probs, values[:seen, :], preferred_element_type=F32
            ).astype(BF16)

    for i in range(1, plane_n):
        exchange(plane_sum, me, plane_peer(i)[1], plane_send.at[i], plane_recv).wait_send()
    for i in range(1, tensor_n):
        dev = line_peer(i)[1]
        exchange(line_sum, z, dev, line_send.at[i], line_recv).wait_send()
        exchange(row_sum, z, dev, row_send.at[i], row_recv).wait_send()

    @pl.when(z != owner)
    def _():
        to_hub(0).wait_send()
        to_hub(1).wait_send()

    @pl.loop(0, tensor_n)
    def _(t):
        for r in range(hubs):
            for part in range(2):
                forwards(r, t, part, wait_send)

    @pl.loop(0, blocks)
    def _(b):
        low, high = span(b)

        @pl.loop(0, chunks)
        def _(c):
            @pl.when(z < high)
            def _():
                chain_up(b, c).wait_send()

            @pl.when(z > low)
            def _():
                chain_down(b, c).wait_send()


def shards(sizes, activations, norm_gain, master_weight, grad, moment, variance, query_gain, key_gain, prompt_len):
    group_n, dp_n, tensor_n = sizes
    plane_n = group_n * dp_n
    hubs = plane_n // tensor_n
    width = norm_gain.shape[0]
    length, feat = activations.shape
    slab_rows, _, slots, head = master_weight.shape
    pair = 2 * head
    blocks = 3 * tensor_n // 2
    chunk = 256 if length % 256 == 0 else length
    chunks = length // chunk
    cosine, sine = rope_tables(length, head)

    def flat(array):
        return array.reshape(slab_rows * slots, head)

    hbm = pl.BlockSpec(memory_space=pl.ANY)
    vmem = pl.BlockSpec(memory_space=pltpu.VMEM)
    dma = pltpu.SemaphoreType.DMA
    return pl.pallas_call(
        functools.partial(kernel, (group_n, dp_n, tensor_n, width)),
        out_shape=jax.ShapeDtypeStruct((length, pair), BF16),
        in_specs=[hbm, vmem, hbm, hbm, hbm, hbm, vmem, vmem, vmem, vmem, pl.BlockSpec(memory_space=pltpu.SMEM)],
        out_specs=vmem,
        scratch_shapes=[
            pltpu.VMEM((length, feat), BF16),
            pltpu.VMEM((length, feat), BF16),
            pltpu.VMEM((slab_rows * slots, head), F32),
            pltpu.VMEM((slots, slab_rows, head), BF16),
            pltpu.VMEM((slab_rows * slots, head), F32),
            pltpu.VMEM((slab_rows * slots, head), F32),
            pltpu.VMEM((slab_rows, pair), BF16),
            pltpu.VMEM((slab_rows, head), BF16),
            pltpu.VMEM((blocks, feat, pair), BF16),
            pltpu.VMEM((blocks, length, pair), F32),
            pltpu.VMEM((blocks, length, pair), BF16),
            pltpu.VMEM((blocks, length, pair), BF16),
            pltpu.VMEM((2, length, pair), F32),
            pltpu.VMEM((2, length, head), BF16),
            pltpu.VMEM((length, head), BF16),
            pltpu.VMEM((length, head), BF16),
            pltpu.VMEM((plane_n, 8, head), F32),
            pltpu.VMEM((tensor_n, 8, head), F32),
            pltpu.VMEM((tensor_n, 8, length), F32),
            dma((5,)),
            dma((plane_n,)),
            dma((plane_n,)),
            dma((tensor_n,)),
            dma((tensor_n,)),
            dma((tensor_n,)),
            dma((tensor_n,)),
            dma((2,)),
            dma((hubs, tensor_n, 2)),
            dma((hubs, tensor_n, 2, group_n // 2 + dp_n - 1)),
            dma((blocks, chunks)),
            dma((blocks, chunks)),
            dma((blocks, chunks)),
            dma((blocks, chunks)),
        ],
        compiler_params=pltpu.CompilerParams(
            collective_id=0, has_side_effects=True, vmem_limit_bytes=60 * 1024 * 1024
        ),
        name="step_and_prefill",
    )(
        activations,
        norm_gain.reshape(tensor_n, 1, feat),
        flat(master_weight),
        jnp.transpose(grad.reshape(slab_rows, slots, head), (1, 0, 2)),
        flat(moment),
        flat(variance),
        query_gain,
        key_gain,
        cosine,
        sine,
        prompt_len,
    )


def solution(mesh):
    in_specs = (
        P(("group", "dp"), "tensor"),
        P(),
        P(("group", "dp"), "tensor", None, None),
        P(("group", "dp"), "tensor", None, None),
        P(("group", "dp"), "tensor", None, None),
        P(("group", "dp"), "tensor", None, None),
        P("tensor", None),
        P(),
        P(("group", "dp")),
    )
    out_specs = P(("group", "dp"), "tensor")
    sizes = tuple(mesh.shape[axis] for axis in ("group", "dp", "tensor"))
    return jax.shard_map(
        functools.partial(shards, sizes), mesh=mesh, in_specs=in_specs, out_specs=out_specs, check_vma=False
    )
```

```python
import functools

import jax
import jax.numpy as jnp
import numpy as np
from jax import lax
from jax.experimental import pallas as pl
from jax.experimental.pallas import tpu as pltpu
from jax.sharding import PartitionSpec as P

STEP_SCALE = 0.5
BETA_ONE = 0.9
BETA_TWO = 0.95
ROPE_BASE = 500000.0
MESH = pl.DeviceIdType.MESH
BF16 = jnp.bfloat16
F32 = jnp.float32


def rope_tables(length, head_size):
    positions = np.arange(length, dtype=np.float32)
    exponent = np.arange(head_size // 2, dtype=np.float32) * np.float32(2.0) / np.float32(head_size)
    inverse = np.power(np.float32(ROPE_BASE), -exponent).astype(np.float32)
    angles = (positions[:, None] * inverse[None, :]).astype(np.float32)
    cosine, sine = np.cos(angles), np.sin(angles)
    return (
        np.concatenate([cosine, cosine], axis=1).astype(np.float32),
        np.concatenate([-sine, sine], axis=1).astype(np.float32),
    )


def kernel(
    sizes,
    act_hbm, gain_ref, master_hbm, grad_hbm, moment_hbm, variance_hbm, query_gain_ref, key_gain_ref,
    cos_ref, sin_ref, len_ref,
    out_ref,
    act, normed, master, grad, moment, variance, own, weights, parts, up, down, final, keys, values,
    plane_sum, line_sum, row_sum,
    in_sem, plane_send, plane_recv, line_send, line_recv, row_send, row_recv,
    hub_send, w_recv, w_send, up_send, up_recv, down_send, down_recv,
):
    group_n, dp_n, tensor_n, width = sizes
    plane_n = group_n * dp_n
    chip_n = group_n // 2
    hubs = plane_n // tensor_n
    length, feat = act.shape
    slab_rows = grad.shape[1]
    blocks = weights.shape[0]
    head = 128
    chunk = 256 if length % 256 == 0 else length
    chunks = length // chunk
    piece_rows = chunk // 2
    pieces = length // piece_rows

    g = lax.axis_index("group")
    d = lax.axis_index("dp")
    z = lax.axis_index("tensor")
    me = g * dp_n + d
    x, core = g // 2, g % 2

    def plane_peer(i):
        p = (me + i) % plane_n
        return p, (p // dp_n, p % dp_n, z)

    def line_peer(i):
        t = (z + i) % tensor_n
        return t, (g, d, t)

    loads = [
        pltpu.make_async_copy(src, dst, in_sem.at[i])
        for i, (src, dst) in enumerate(
            [(grad_hbm, grad), (act_hbm, act), (moment_hbm, moment), (variance_hbm, variance), (master_hbm, master)]
        )
    ]
    for load in loads:
        load.start()

    barrier = pltpu.get_barrier_semaphore()
    for i in range(1, plane_n):
        pl.semaphore_signal(barrier, inc=1, device_id=plane_peer(i)[1], device_id_type=MESH)
    for i in range(1, tensor_n):
        pl.semaphore_signal(barrier, inc=1, device_id=line_peer(i)[1], device_id_type=MESH)

    loads[0].wait()
    tile = jnp.zeros((8, head), F32)
    for s in range(3):
        piece = grad[s].astype(F32)
        tile += jnp.sum((piece * piece).reshape(slab_rows // 8, 8, head), axis=0)
    plane_sum[me] = tile
    pl.semaphore_wait(barrier, plane_n + tensor_n - 2)

    def exchange(buf, slot, dev, ssem, rsem):
        return pltpu.make_async_remote_copy(
            src_ref=buf.at[slot], dst_ref=buf.at[slot], send_sem=ssem, recv_sem=rsem.at[slot],
            device_id=dev, device_id_type=MESH,
        )

    for i in range(1, plane_n):
        exchange(plane_sum, me, plane_peer(i)[1], plane_send.at[i], plane_recv).start()

    loads[1].wait()
    for c in range(chunks):
        rows = pl.ds(c * chunk, chunk)
        wide = act[rows, :].astype(F32)
        column = jnp.sum(wide * wide, axis=1, keepdims=True)
        row_sum[z, :, rows] = jnp.broadcast_to(column, (chunk, head)).T[:8]
    for i in range(1, tensor_n):
        exchange(row_sum, z, line_peer(i)[1], row_send.at[i], row_recv).start()

    total = plane_sum[me]
    for i in range(1, plane_n):
        p, dev = plane_peer(i)
        exchange(plane_sum, p, dev, plane_send.at[i], plane_recv).wait_recv()
        total += plane_sum[p]
    line_sum[z] = total
    for i in range(1, tensor_n):
        exchange(line_sum, z, line_peer(i)[1], line_send.at[i], line_recv).start()
    for load in loads[2:]:
        load.wait()
    for i in range(1, tensor_n):
        t, dev = line_peer(i)
        exchange(line_sum, t, dev, line_send.at[i], line_recv).wait_recv()
        total += line_sum[t]
    sumsq = jnp.sum(jnp.sum(total, axis=0, keepdims=True), axis=1, keepdims=True)
    clip = 1.0 / jnp.sqrt(sumsq + 1e-12)

    step_size = STEP_SCALE * width ** (-0.5)

    def updated(s):
        clipped = grad[s].astype(F32) * clip
        rows = pl.ds(s, slab_rows, stride=3)
        moment_new = BETA_ONE * moment[rows, :] + (1.0 - BETA_ONE) * clipped
        variance_new = BETA_TWO * variance[rows, :] + (1.0 - BETA_TWO) * clipped * clipped
        return (master[rows, :] - step_size * moment_new / (jnp.sqrt(variance_new) + 1e-08)).astype(BF16)

    def q_block(t):
        return 3 * (t // 2) + 2 * (t % 2)

    def kv_block(t):
        return 3 * (t // 2) + 1

    def w_slot(r, t, part):
        rows = pl.ds(pl.multiple_of(r * slab_rows, 16), slab_rows)
        if part < 2:
            return weights.at[q_block(t), rows, part * head : (part + 1) * head]
        return weights.at[kv_block(t), rows, pl.ds(pl.multiple_of((t % 2) * head, head), head)]

    owner, my_r = me // hubs, me % hubs

    def to_hub(part):
        return pltpu.make_async_remote_copy(
            src_ref=own.at[part], dst_ref=w_slot(my_r, z, part), send_sem=hub_send.at[part],
            recv_sem=w_recv.at[my_r, z, part], device_id=(g, d, owner), device_id_type=MESH,
        )

    def place(part):
        @pl.when(z == owner)
        def _():
            w_slot(my_r, z, part)[...] = own[part]

        @pl.when(z != owner)
        def _():
            to_hub(part).start()

    for part in range(3):
        own[part] = updated(part)
        place(part)

    square = row_sum[z]
    for i in range(1, tensor_n):
        t, dev = line_peer(i)
        exchange(row_sum, t, dev, row_send.at[i], row_recv).wait_recv()
        square += row_sum[t]
    scale_row = lax.rsqrt(square[:1] * (1.0 / width) + 1e-06)
    for c in range(chunks):
        rows = pl.ds(c * chunk, chunk)
        scale = jnp.broadcast_to(scale_row[:, c * chunk : (c + 1) * chunk], (head, chunk)).T[:, :1]
        normed[rows, :] = (act[rows, :].astype(F32) * scale * gain_ref[z]).astype(BF16)

    def forward(r, t, part, slot, dev):
        return pltpu.make_async_remote_copy(
            src_ref=w_slot(r, t, part), dst_ref=w_slot(r, t, part), send_sem=w_send.at[r, t, part, slot],
            recv_sem=w_recv.at[r, t, part], device_id=dev, device_id_type=MESH,
        )

    def forwards(r, t, part, act_on):
        hub = z * hubs + r
        hub_g, hub_d = hub // dp_n, hub % dp_n
        same_core = core == hub_g % 2
        at_hub = hub == me

        @pl.when(at_hub)
        def _():
            for i in range(1, chip_n):
                act_on(forward(r, t, part, i - 1, (((x + i) % chip_n) * 2 + core, d, z)))

        @pl.when(jnp.logical_and(same_core, d == hub_d))
        def _():
            for i in range(1, dp_n):
                act_on(forward(r, t, part, chip_n - 2 + i, (g, (d + i) % dp_n, z)))

        @pl.when(same_core)
        def _():
            act_on(forward(r, t, part, chip_n + dp_n - 2, (x * 2 + 1 - core, d, z)))

    def start(copy):
        copy.start()

    def wait_send(copy):
        copy.wait_send()

    def chain(buf, b, c, dev_z, ssem, rsem):
        rows = pl.ds(pl.multiple_of(c * piece_rows, 16), piece_rows)
        return pltpu.make_async_remote_copy(
            src_ref=buf.at[b, rows, :], dst_ref=buf.at[b, rows, :], send_sem=ssem.at[b, c], recv_sem=rsem.at[b, c],
            device_id=(g, d, dev_z), device_id_type=MESH,
        )

    def chain_up(b, c):
        return chain(up, b, c, jnp.minimum(z + 1, tensor_n - 1), up_send, up_recv)

    def chain_down(b, c):
        return chain(down, b, c, jnp.maximum(z - 1, 0), down_send, down_recv)

    def span(b):
        pair, j = b // 3, b % 3
        return 2 * pair + j // 2, 2 * pair + (j + 1) // 2

    def multiply(*todo):
        @pl.loop(0, chunks)
        def _(c):
            rows = pl.ds(pl.multiple_of(c * chunk, 16), chunk)
            for b in todo:
                low, high = span(b)
                parts[b, rows, :] = jnp.dot(normed[rows, :], weights[b], preferred_element_type=F32)

                @pl.when(jnp.logical_and(z == 0, z < high))
                def _():
                    up[b, rows, :] = parts[b, rows, :].astype(BF16)
                    for half in range(2):
                        chain_up(b, 2 * c + half).start()

                @pl.when(jnp.logical_and(z == tensor_n - 1, z > low))
                def _():
                    down[b, rows, :] = parts[b, rows, :].astype(BF16)
                    for half in range(2):
                        chain_down(b, 2 * c + half).start()

    @pl.loop(0, 2 * tensor_n - 1)
    def _(k):
        distance = (k + 1) // 2
        t = z + distance * (2 * (k % 2) - 1)

        @pl.when(jnp.logical_and(t >= 0, t < tensor_n))
        def _():
            for i in range(hubs):
                r = (d + i) % hubs
                for part in range(3):
                    @pl.when(jnp.logical_not(jnp.logical_and(z * hubs + r == me, t == z)))
                    def _():
                        forward(r, t, part, 0, (g, d, z)).wait_recv()

                    forwards(r, t, part, start)
            mate = t + 1 - 2 * (t % 2)
            offset = mate - z
            rank = jnp.where(offset > 0, 2 * offset - 1, -2 * offset)

            @pl.when(rank < k)
            def _():
                multiply(kv_block(t), q_block(t))

            @pl.when(rank >= k)
            def _():
                multiply(q_block(t))

    mine = (q_block(z), kv_block(z))
    for slot in range(2):
        final[slot] = parts[mine[slot]]

    def hop(b, c, buf, copy, receives, sends):
        low, high = span(b)
        rows = pl.ds(pl.multiple_of(c * piece_rows, 16), piece_rows)

        @pl.when(receives)
        def _():
            copy(b, c).wait_recv()
            arrived = buf[b, rows, :].astype(F32)

            @pl.when(sends)
            def _():
                buf[b, rows, :] = (parts[b, rows, :] + arrived).astype(BF16)
                copy(b, c).start()

            @pl.when(jnp.logical_and(low <= z, z <= high))
            def _():
                slot = 1 - abs(b % 3 - 1)
                final[slot, rows, :] += arrived

    def hop_up(b, c):
        high = span(b)[1]
        hop(b, c, up, chain_up, jnp.logical_and(z > 0, z <= high), z < high)

    def hop_down(b, c):
        low = span(b)[0]
        hop(b, c, down, chain_down, jnp.logical_and(z < tensor_n - 1, z >= low), z > low)

    @pl.loop(0, blocks - 2)
    def _(i):
        @pl.loop(0, pieces)
        def _(c):
            hop_up(i, c)
            hop_down(blocks - 1 - i, c)

    def prepared(raw, gains, rows):
        scaled = raw * lax.rsqrt(jnp.mean(raw * raw, axis=1, keepdims=True) + 1e-06) * gains
        return scaled * cos_ref[rows, :] + pltpu.roll(scaled, head // 2, 1) * sin_ref[rows, :]

    key_gain = key_gain_ref[pl.ds(z // 2, 1), :]
    live = len_ref[0]
    for c in range(chunks):
        @pl.loop(2 * c, 2 * c + 2)
        def _(p):
            for i in range(2):
                hop_up(blocks - 2 + i, p)
                hop_down(1 - i, p)

        rows = pl.ds(c * chunk, chunk)
        seen = (c + 1) * chunk
        keys[rows, :] = prepared(final[1, rows, :head], key_gain, rows).astype(BF16)
        values[rows, :] = final[1, rows, head:].astype(BF16)
        row_pos = lax.broadcasted_iota(jnp.int32, (chunk, seen), 0) + c * chunk
        col_pos = lax.broadcasted_iota(jnp.int32, (chunk, seen), 1)
        allowed = jnp.logical_and(col_pos <= row_pos, col_pos < live)
        for j in range(2):
            raw = final[0, rows, j * head : (j + 1) * head]
            query = (prepared(raw, query_gain_ref[j : j + 1, :], rows) * head ** (-0.5)).astype(BF16)
            scores = lax.dot_general(query, keys[:seen, :], (((1,), (1,)), ((), ())), preferred_element_type=F32)
            scores = jnp.where(allowed, scores, -1e30)
            exps = jnp.exp(scores - jnp.max(scores, axis=1, keepdims=True))
            probs = (exps / jnp.sum(exps, axis=1, keepdims=True)).astype(BF16)
            out_ref[rows, j * head : (j + 1) * head] = jnp.dot(
                probs, values[:seen, :], preferred_element_type=F32
            ).astype(BF16)

    for i in range(1, plane_n):
        exchange(plane_sum, me, plane_peer(i)[1], plane_send.at[i], plane_recv).wait_send()
    for i in range(1, tensor_n):
        dev = line_peer(i)[1]
        exchange(line_sum, z, dev, line_send.at[i], line_recv).wait_send()
        exchange(row_sum, z, dev, row_send.at[i], row_recv).wait_send()

    @pl.when(z != owner)
    def _():
        for part in range(3):
            to_hub(part).wait_send()

    @pl.loop(0, tensor_n)
    def _(t):
        for r in range(hubs):
            for part in range(3):
                forwards(r, t, part, wait_send)

    @pl.loop(0, blocks)
    def _(b):
        low, high = span(b)

        @pl.loop(0, pieces)
        def _(c):
            @pl.when(z < high)
            def _():
                chain_up(b, c).wait_send()

            @pl.when(z > low)
            def _():
                chain_down(b, c).wait_send()


def shards(sizes, activations, norm_gain, master_weight, grad, moment, variance, query_gain, key_gain, prompt_len):
    group_n, dp_n, tensor_n = sizes
    plane_n = group_n * dp_n
    hubs = plane_n // tensor_n
    width = norm_gain.shape[0]
    length, feat = activations.shape
    slab_rows, _, slots, head = master_weight.shape
    pair = 2 * head
    blocks = 3 * tensor_n // 2
    chunk = 256 if length % 256 == 0 else length
    pieces = 2 * (length // chunk)
    cosine, sine = rope_tables(length, head)

    def flat(array):
        return array.reshape(slab_rows * slots, head)

    hbm = pl.BlockSpec(memory_space=pl.ANY)
    vmem = pl.BlockSpec(memory_space=pltpu.VMEM)
    dma = pltpu.SemaphoreType.DMA
    return pl.pallas_call(
        functools.partial(kernel, (group_n, dp_n, tensor_n, width)),
        out_shape=jax.ShapeDtypeStruct((length, pair), BF16),
        in_specs=[hbm, vmem, hbm, hbm, hbm, hbm, vmem, vmem, vmem, vmem, pl.BlockSpec(memory_space=pltpu.SMEM)],
        out_specs=vmem,
        scratch_shapes=[
            pltpu.VMEM((length, feat), BF16),
            pltpu.VMEM((length, feat), BF16),
            pltpu.VMEM((slab_rows * slots, head), F32),
            pltpu.VMEM((slots, slab_rows, head), BF16),
            pltpu.VMEM((slab_rows * slots, head), F32),
            pltpu.VMEM((slab_rows * slots, head), F32),
            pltpu.VMEM((slots, slab_rows, head), BF16),
            pltpu.VMEM((blocks, feat, pair), BF16),
            pltpu.VMEM((blocks, length, pair), F32),
            pltpu.VMEM((blocks, length, pair), BF16),
            pltpu.VMEM((blocks, length, pair), BF16),
            pltpu.VMEM((2, length, pair), F32),
            pltpu.VMEM((length, head), BF16),
            pltpu.VMEM((length, head), BF16),
            pltpu.VMEM((plane_n, 8, head), F32),
            pltpu.VMEM((tensor_n, 8, head), F32),
            pltpu.VMEM((tensor_n, 8, length), F32),
            dma((5,)),
            dma((plane_n,)),
            dma((plane_n,)),
            dma((tensor_n,)),
            dma((tensor_n,)),
            dma((tensor_n,)),
            dma((tensor_n,)),
            dma((3,)),
            dma((hubs, tensor_n, 3)),
            dma((hubs, tensor_n, 3, group_n // 2 + dp_n - 1)),
            dma((blocks, pieces)),
            dma((blocks, pieces)),
            dma((blocks, pieces)),
            dma((blocks, pieces)),
        ],
        compiler_params=pltpu.CompilerParams(
            collective_id=0, has_side_effects=True, vmem_limit_bytes=60 * 1024 * 1024
        ),
        name="step_and_prefill",
    )(
        activations,
        norm_gain.reshape(tensor_n, 1, feat),
        flat(master_weight),
        jnp.transpose(grad.reshape(slab_rows, slots, head), (1, 0, 2)),
        flat(moment),
        flat(variance),
        query_gain,
        key_gain,
        cosine,
        sine,
        prompt_len,
    )


def solution(mesh):
    in_specs = (
        P(("group", "dp"), "tensor"),
        P(),
        P(("group", "dp"), "tensor", None, None),
        P(("group", "dp"), "tensor", None, None),
        P(("group", "dp"), "tensor", None, None),
        P(("group", "dp"), "tensor", None, None),
        P("tensor", None),
        P(),
        P(("group", "dp")),
    )
    out_specs = P(("group", "dp"), "tensor")
    sizes = tuple(mesh.shape[axis] for axis in ("group", "dp", "tensor"))
    return jax.shard_map(
        functools.partial(shards, sizes), mesh=mesh, in_specs=in_specs, out_specs=out_specs, check_vma=False
    )
```

```python
import functools

import jax
import jax.numpy as jnp
import numpy as np
from jax import lax
from jax.experimental import pallas as pl
from jax.experimental.pallas import tpu as pltpu
from jax.sharding import PartitionSpec as P

STEP_SCALE = 0.5
BETA_ONE = 0.9
BETA_TWO = 0.95
ROPE_BASE = 500000.0
MESH = pl.DeviceIdType.MESH
BF16 = jnp.bfloat16
F32 = jnp.float32


def rope_tables(length, head_size):
    positions = np.arange(length, dtype=np.float32)
    exponent = np.arange(head_size // 2, dtype=np.float32) * np.float32(2.0) / np.float32(head_size)
    inverse = np.power(np.float32(ROPE_BASE), -exponent).astype(np.float32)
    angles = (positions[:, None] * inverse[None, :]).astype(np.float32)
    cosine, sine = np.cos(angles), np.sin(angles)
    return (
        np.concatenate([cosine, cosine], axis=1).astype(np.float32),
        np.concatenate([-sine, sine], axis=1).astype(np.float32),
    )


def kernel(
    sizes,
    act_hbm, gain_ref, master_hbm, grad_hbm, moment_hbm, variance_hbm, query_gain_ref, key_gain_ref,
    cos_ref, sin_ref, len_ref,
    out_ref,
    act, normed, master, grad, moment, variance, own, weights, parts, up, down, final, keys, values,
    plane_sum, line_sum, row_sum,
    in_sem, plane_send, plane_recv, line_send, line_recv, row_send, row_recv,
    hub_send, w_recv, w_send, up_send, up_recv, down_send, down_recv,
):
    group_n, dp_n, tensor_n, width = sizes
    plane_n = group_n * dp_n
    chip_n = group_n // 2
    hubs = plane_n // tensor_n
    length, feat = act.shape
    slab_rows = grad.shape[1]
    blocks = weights.shape[0] // 2
    head = 128
    chunk = 256 if length % 256 == 0 else length
    chunks = length // chunk
    piece_rows = chunk // 2
    pieces = length // piece_rows

    g = lax.axis_index("group")
    d = lax.axis_index("dp")
    z = lax.axis_index("tensor")
    me = g * dp_n + d
    x, core = g // 2, g % 2

    def plane_peer(i):
        p = (me + i) % plane_n
        return p, (p // dp_n, p % dp_n, z)

    def line_peer(i):
        t = (z + i) % tensor_n
        return t, (g, d, t)

    loads = [
        pltpu.make_async_copy(src, dst, in_sem.at[i])
        for i, (src, dst) in enumerate(
            [(grad_hbm, grad), (act_hbm, act), (moment_hbm, moment), (variance_hbm, variance), (master_hbm, master)]
        )
    ]
    for load in loads:
        load.start()

    barrier = pltpu.get_barrier_semaphore()
    for i in range(1, plane_n):
        pl.semaphore_signal(barrier, inc=1, device_id=plane_peer(i)[1], device_id_type=MESH)
    for i in range(1, tensor_n):
        pl.semaphore_signal(barrier, inc=1, device_id=line_peer(i)[1], device_id_type=MESH)

    loads[0].wait()
    tile = jnp.zeros((8, head), F32)
    for s in range(3):
        piece = grad[s].astype(F32)
        tile += jnp.sum((piece * piece).reshape(slab_rows // 8, 8, head), axis=0)
    plane_sum[me] = tile
    pl.semaphore_wait(barrier, plane_n + tensor_n - 2)

    def exchange(buf, slot, dev, ssem, rsem):
        return pltpu.make_async_remote_copy(
            src_ref=buf.at[slot], dst_ref=buf.at[slot], send_sem=ssem, recv_sem=rsem.at[slot],
            device_id=dev, device_id_type=MESH,
        )

    for i in range(1, plane_n):
        exchange(plane_sum, me, plane_peer(i)[1], plane_send.at[i], plane_recv).start()

    loads[1].wait()
    for c in range(chunks):
        rows = pl.ds(c * chunk, chunk)
        wide = act[rows, :].astype(F32)
        column = jnp.sum(wide * wide, axis=1, keepdims=True)
        row_sum[z, :, rows] = jnp.broadcast_to(column, (chunk, head)).T[:8]
    for i in range(1, tensor_n):
        exchange(row_sum, z, line_peer(i)[1], row_send.at[i], row_recv).start()

    total = plane_sum[me]
    for i in range(1, plane_n):
        p, dev = plane_peer(i)
        exchange(plane_sum, p, dev, plane_send.at[i], plane_recv).wait_recv()
        total += plane_sum[p]
    line_sum[z] = total
    for i in range(1, tensor_n):
        exchange(line_sum, z, line_peer(i)[1], line_send.at[i], line_recv).start()
    for load in loads[2:]:
        load.wait()
    for i in range(1, tensor_n):
        t, dev = line_peer(i)
        exchange(line_sum, t, dev, line_send.at[i], line_recv).wait_recv()
        total += line_sum[t]
    sumsq = jnp.sum(jnp.sum(total, axis=0, keepdims=True), axis=1, keepdims=True)
    clip = 1.0 / jnp.sqrt(sumsq + 1e-12)

    step_size = STEP_SCALE * width ** (-0.5)

    def updated(s):
        clipped = grad[s].astype(F32) * clip
        rows = pl.ds(s, slab_rows, stride=3)
        moment_new = BETA_ONE * moment[rows, :] + (1.0 - BETA_ONE) * clipped
        variance_new = BETA_TWO * variance[rows, :] + (1.0 - BETA_TWO) * clipped * clipped
        return (master[rows, :] - step_size * moment_new / (jnp.sqrt(variance_new) + 1e-08)).astype(BF16)

    def q_block(t):
        return 3 * (t // 2) + 2 * (t % 2)

    def kv_block(t):
        return 3 * (t // 2) + 1

    def w_slot(r, t, part):
        rows = pl.ds(pl.multiple_of(r * slab_rows, 16), slab_rows)
        column = 2 * q_block(t) + part if part < 2 else 2 * kv_block(t) + t % 2
        return weights.at[column, rows, :]

    owner, my_r = me // hubs, me % hubs

    def to_hub(part):
        return pltpu.make_async_remote_copy(
            src_ref=own.at[part], dst_ref=w_slot(my_r, z, part), send_sem=hub_send.at[part],
            recv_sem=w_recv.at[my_r, z, part], device_id=(g, d, owner), device_id_type=MESH,
        )

    def place(part):
        @pl.when(z == owner)
        def _():
            w_slot(my_r, z, part)[...] = own[part]

        @pl.when(z != owner)
        def _():
            to_hub(part).start()

    for part in range(3):
        own[part] = updated(part)
        place(part)

    square = row_sum[z]
    for i in range(1, tensor_n):
        t, dev = line_peer(i)
        exchange(row_sum, t, dev, row_send.at[i], row_recv).wait_recv()
        square += row_sum[t]
    scale_row = lax.rsqrt(square[:1] * (1.0 / width) + 1e-06)
    for c in range(chunks):
        rows = pl.ds(c * chunk, chunk)
        scale = jnp.broadcast_to(scale_row[:, c * chunk : (c + 1) * chunk], (head, chunk)).T[:, :1]
        normed[rows, :] = (act[rows, :].astype(F32) * scale * gain_ref[z]).astype(BF16)

    def forward(r, t, part, slot, dev):
        return pltpu.make_async_remote_copy(
            src_ref=w_slot(r, t, part), dst_ref=w_slot(r, t, part), send_sem=w_send.at[r, t, part, slot],
            recv_sem=w_recv.at[r, t, part], device_id=dev, device_id_type=MESH,
        )

    def forwards(r, t, part, act_on):
        hub = z * hubs + r
        hub_g, hub_d = hub // dp_n, hub % dp_n
        same_core = core == hub_g % 2
        at_hub = hub == me

        @pl.when(at_hub)
        def _():
            for i in range(1, chip_n):
                act_on(forward(r, t, part, i - 1, (((x + i) % chip_n) * 2 + core, d, z)))

        @pl.when(jnp.logical_and(same_core, d == hub_d))
        def _():
            for i in range(1, dp_n):
                act_on(forward(r, t, part, chip_n - 2 + i, (g, (d + i) % dp_n, z)))

        @pl.when(same_core)
        def _():
            act_on(forward(r, t, part, chip_n + dp_n - 2, (x * 2 + 1 - core, d, z)))

    def start(copy):
        copy.start()

    def wait_send(copy):
        copy.wait_send()

    def chain(buf, b, c, dev_z, ssem, rsem):
        rows = pl.ds(pl.multiple_of(c * piece_rows, 16), piece_rows)
        return pltpu.make_async_remote_copy(
            src_ref=buf.at[b, rows, :], dst_ref=buf.at[b, rows, :], send_sem=ssem.at[b, c], recv_sem=rsem.at[b, c],
            device_id=(g, d, dev_z), device_id_type=MESH,
        )

    def chain_up(b, c):
        return chain(up, b, c, jnp.minimum(z + 1, tensor_n - 1), up_send, up_recv)

    def chain_down(b, c):
        return chain(down, b, c, jnp.maximum(z - 1, 0), down_send, down_recv)

    def span(b):
        pair, j = b // 3, b % 3
        return 2 * pair + j // 2, 2 * pair + (j + 1) // 2

    def multiply(*todo):
        @pl.loop(0, chunks)
        def _(c):
            rows = pl.ds(pl.multiple_of(c * chunk, 16), chunk)
            for b in todo:
                low, high = span(b)
                both = jnp.concatenate([weights[2 * b], weights[2 * b + 1]], axis=1)
                parts[b, rows, :] = jnp.dot(normed[rows, :], both, preferred_element_type=F32)

                @pl.when(jnp.logical_and(z == 0, z < high))
                def _():
                    up[b, rows, :] = parts[b, rows, :].astype(BF16)
                    for half in range(2):
                        chain_up(b, 2 * c + half).start()

                @pl.when(jnp.logical_and(z == tensor_n - 1, z > low))
                def _():
                    down[b, rows, :] = parts[b, rows, :].astype(BF16)
                    for half in range(2):
                        chain_down(b, 2 * c + half).start()

    @pl.loop(0, 2 * tensor_n - 1)
    def _(k):
        distance = (k + 1) // 2
        t = z + distance * (2 * (k % 2) - 1)

        @pl.when(jnp.logical_and(t >= 0, t < tensor_n))
        def _():
            for i in range(hubs):
                r = (d + i) % hubs
                for part in range(3):
                    @pl.when(jnp.logical_not(jnp.logical_and(z * hubs + r == me, t == z)))
                    def _():
                        forward(r, t, part, 0, (g, d, z)).wait_recv()

                    forwards(r, t, part, start)
            mate = t + 1 - 2 * (t % 2)
            offset = mate - z
            rank = jnp.where(offset > 0, 2 * offset - 1, -2 * offset)

            @pl.when(rank < k)
            def _():
                multiply(kv_block(t), q_block(t))

            @pl.when(rank >= k)
            def _():
                multiply(q_block(t))

    mine = (q_block(z), kv_block(z))
    for slot in range(2):
        final[slot] = parts[mine[slot]]

    def hop(b, c, buf, copy, receives, sends):
        low, high = span(b)
        rows = pl.ds(pl.multiple_of(c * piece_rows, 16), piece_rows)

        @pl.when(receives)
        def _():
            copy(b, c).wait_recv()
            arrived = buf[b, rows, :].astype(F32)

            @pl.when(sends)
            def _():
                buf[b, rows, :] = (parts[b, rows, :] + arrived).astype(BF16)
                copy(b, c).start()

            @pl.when(jnp.logical_and(low <= z, z <= high))
            def _():
                slot = 1 - abs(b % 3 - 1)
                final[slot, rows, :] += arrived

    def hop_up(b, c):
        high = span(b)[1]
        hop(b, c, up, chain_up, jnp.logical_and(z > 0, z <= high), z < high)

    def hop_down(b, c):
        low = span(b)[0]
        hop(b, c, down, chain_down, jnp.logical_and(z < tensor_n - 1, z >= low), z > low)

    @pl.loop(0, blocks - 2)
    def _(i):
        @pl.loop(0, pieces)
        def _(c):
            hop_up(i, c)
            hop_down(blocks - 1 - i, c)

    def prepared(raw, gains, rows):
        scaled = raw * lax.rsqrt(jnp.mean(raw * raw, axis=1, keepdims=True) + 1e-06) * gains
        return scaled * cos_ref[rows, :] + pltpu.roll(scaled, head // 2, 1) * sin_ref[rows, :]

    key_gain = key_gain_ref[pl.ds(z // 2, 1), :]
    live = len_ref[0]
    for c in range(chunks):
        @pl.loop(2 * c, 2 * c + 2)
        def _(p):
            for i in range(2):
                hop_up(blocks - 2 + i, p)
                hop_down(1 - i, p)

        rows = pl.ds(c * chunk, chunk)
        seen = (c + 1) * chunk
        keys[rows, :] = prepared(final[1, rows, :head], key_gain, rows).astype(BF16)
        values[rows, :] = final[1, rows, head:].astype(BF16)
        row_pos = lax.broadcasted_iota(jnp.int32, (chunk, seen), 0) + c * chunk
        col_pos = lax.broadcasted_iota(jnp.int32, (chunk, seen), 1)
        allowed = jnp.logical_and(col_pos <= row_pos, col_pos < live)
        for j in range(2):
            raw = final[0, rows, j * head : (j + 1) * head]
            query = (prepared(raw, query_gain_ref[j : j + 1, :], rows) * head ** (-0.5)).astype(BF16)
            scores = lax.dot_general(query, keys[:seen, :], (((1,), (1,)), ((), ())), preferred_element_type=F32)
            scores = jnp.where(allowed, scores, -1e30)
            exps = jnp.exp(scores - jnp.max(scores, axis=1, keepdims=True))
            probs = (exps / jnp.sum(exps, axis=1, keepdims=True)).astype(BF16)
            out_ref[rows, j * head : (j + 1) * head] = jnp.dot(
                probs, values[:seen, :], preferred_element_type=F32
            ).astype(BF16)

    for i in range(1, plane_n):
        exchange(plane_sum, me, plane_peer(i)[1], plane_send.at[i], plane_recv).wait_send()
    for i in range(1, tensor_n):
        dev = line_peer(i)[1]
        exchange(line_sum, z, dev, line_send.at[i], line_recv).wait_send()
        exchange(row_sum, z, dev, row_send.at[i], row_recv).wait_send()

    @pl.when(z != owner)
    def _():
        for part in range(3):
            to_hub(part).wait_send()

    @pl.loop(0, tensor_n)
    def _(t):
        for r in range(hubs):
            for part in range(3):
                forwards(r, t, part, wait_send)

    @pl.loop(0, blocks)
    def _(b):
        low, high = span(b)

        @pl.loop(0, pieces)
        def _(c):
            @pl.when(z < high)
            def _():
                chain_up(b, c).wait_send()

            @pl.when(z > low)
            def _():
                chain_down(b, c).wait_send()


def shards(sizes, activations, norm_gain, master_weight, grad, moment, variance, query_gain, key_gain, prompt_len):
    group_n, dp_n, tensor_n = sizes
    plane_n = group_n * dp_n
    hubs = plane_n // tensor_n
    width = norm_gain.shape[0]
    length, feat = activations.shape
    slab_rows, _, slots, head = master_weight.shape
    pair = 2 * head
    blocks = 3 * tensor_n // 2
    chunk = 256 if length % 256 == 0 else length
    pieces = 2 * (length // chunk)
    cosine, sine = rope_tables(length, head)

    def flat(array):
        return array.reshape(slab_rows * slots, head)

    hbm = pl.BlockSpec(memory_space=pl.ANY)
    vmem = pl.BlockSpec(memory_space=pltpu.VMEM)
    dma = pltpu.SemaphoreType.DMA
    return pl.pallas_call(
        functools.partial(kernel, (group_n, dp_n, tensor_n, width)),
        out_shape=jax.ShapeDtypeStruct((length, pair), BF16),
        in_specs=[hbm, vmem, hbm, hbm, hbm, hbm, vmem, vmem, vmem, vmem, pl.BlockSpec(memory_space=pltpu.SMEM)],
        out_specs=vmem,
        scratch_shapes=[
            pltpu.VMEM((length, feat), BF16),
            pltpu.VMEM((length, feat), BF16),
            pltpu.VMEM((slab_rows * slots, head), F32),
            pltpu.VMEM((slots, slab_rows, head), BF16),
            pltpu.VMEM((slab_rows * slots, head), F32),
            pltpu.VMEM((slab_rows * slots, head), F32),
            pltpu.VMEM((slots, slab_rows, head), BF16),
            pltpu.VMEM((2 * blocks, feat, head), BF16),
            pltpu.VMEM((blocks, length, pair), F32),
            pltpu.VMEM((blocks, length, pair), BF16),
            pltpu.VMEM((blocks, length, pair), BF16),
            pltpu.VMEM((2, length, pair), F32),
            pltpu.VMEM((length, head), BF16),
            pltpu.VMEM((length, head), BF16),
            pltpu.VMEM((plane_n, 8, head), F32),
            pltpu.VMEM((tensor_n, 8, head), F32),
            pltpu.VMEM((tensor_n, 8, length), F32),
            dma((5,)),
            dma((plane_n,)),
            dma((plane_n,)),
            dma((tensor_n,)),
            dma((tensor_n,)),
            dma((tensor_n,)),
            dma((tensor_n,)),
            dma((3,)),
            dma((hubs, tensor_n, 3)),
            dma((hubs, tensor_n, 3, group_n // 2 + dp_n - 1)),
            dma((blocks, pieces)),
            dma((blocks, pieces)),
            dma((blocks, pieces)),
            dma((blocks, pieces)),
        ],
        compiler_params=pltpu.CompilerParams(
            collective_id=0, has_side_effects=True, vmem_limit_bytes=60 * 1024 * 1024
        ),
        name="step_and_prefill",
    )(
        activations,
        norm_gain.reshape(tensor_n, 1, feat),
        flat(master_weight),
        jnp.transpose(grad.reshape(slab_rows, slots, head), (1, 0, 2)),
        flat(moment),
        flat(variance),
        query_gain,
        key_gain,
        cosine,
        sine,
        prompt_len,
    )


def solution(mesh):
    in_specs = (
        P(("group", "dp"), "tensor"),
        P(),
        P(("group", "dp"), "tensor", None, None),
        P(("group", "dp"), "tensor", None, None),
        P(("group", "dp"), "tensor", None, None),
        P(("group", "dp"), "tensor", None, None),
        P("tensor", None),
        P(),
        P(("group", "dp")),
    )
    out_specs = P(("group", "dp"), "tensor")
    sizes = tuple(mesh.shape[axis] for axis in ("group", "dp", "tensor"))
    return jax.shard_map(
        functools.partial(shards, sizes), mesh=mesh, in_specs=in_specs, out_specs=out_specs, check_vma=False
    )
```

```python
import functools

import jax
import jax.numpy as jnp
import numpy as np
from jax import lax
from jax.experimental import pallas as pl
from jax.experimental.pallas import tpu as pltpu
from jax.sharding import PartitionSpec as P

STEP_SCALE = 0.5
BETA_ONE = 0.9
BETA_TWO = 0.95
ROPE_BASE = 500000.0
MESH = pl.DeviceIdType.MESH
BF16 = jnp.bfloat16
F32 = jnp.float32


def rope_tables(length, head_size):
    positions = np.arange(length, dtype=np.float32)
    exponent = np.arange(head_size // 2, dtype=np.float32) * np.float32(2.0) / np.float32(head_size)
    inverse = np.power(np.float32(ROPE_BASE), -exponent).astype(np.float32)
    angles = (positions[:, None] * inverse[None, :]).astype(np.float32)
    cosine, sine = np.cos(angles), np.sin(angles)
    return (
        np.concatenate([cosine, cosine], axis=1).astype(np.float32),
        np.concatenate([-sine, sine], axis=1).astype(np.float32),
    )


def kernel(
    sizes,
    act_hbm, gain_ref, master_hbm, grad_hbm, moment_hbm, variance_hbm, query_gain_ref, key_gain_ref,
    cos_ref, sin_ref, len_ref,
    out_ref,
    act, normed, master, grad, moment, variance, own, weights, parts, up, down, final, keys, values,
    plane_sum, line_sum, row_sum,
    in_sem, plane_send, plane_recv, line_send, line_recv, row_send, row_recv,
    hub_send, w_recv, w_send, up_send, up_recv, down_send, down_recv,
):
    group_n, dp_n, tensor_n, width = sizes
    plane_n = group_n * dp_n
    chip_n = group_n // 2
    hubs = plane_n // tensor_n
    length, feat = act.shape
    slab_rows = grad.shape[1]
    blocks = weights.shape[0] // 2
    head = 128
    chunk = 256 if length % 256 == 0 else length
    chunks = length // chunk
    piece_rows = chunk // 2
    pieces = length // piece_rows

    g = lax.axis_index("group")
    d = lax.axis_index("dp")
    z = lax.axis_index("tensor")
    me = g * dp_n + d
    x, core = g // 2, g % 2

    def plane_peer(i):
        p = (me + i) % plane_n
        return p, (p // dp_n, p % dp_n, z)

    def line_peer(i):
        t = (z + i) % tensor_n
        return t, (g, d, t)

    loads = [
        pltpu.make_async_copy(src, dst, in_sem.at[i])
        for i, (src, dst) in enumerate(
            [(grad_hbm, grad), (act_hbm, act), (moment_hbm, moment), (variance_hbm, variance), (master_hbm, master)]
        )
    ]
    for load in loads:
        load.start()

    barrier = pltpu.get_barrier_semaphore()
    for i in range(1, plane_n):
        pl.semaphore_signal(barrier, inc=1, device_id=plane_peer(i)[1], device_id_type=MESH)
    for i in range(1, tensor_n):
        pl.semaphore_signal(barrier, inc=1, device_id=line_peer(i)[1], device_id_type=MESH)

    loads[0].wait()
    tile = jnp.zeros((8, head), F32)
    for s in range(3):
        piece = grad[s].astype(F32)
        tile += jnp.sum((piece * piece).reshape(slab_rows // 8, 8, head), axis=0)
    plane_sum[me] = tile
    pl.semaphore_wait(barrier, plane_n + tensor_n - 2)

    def exchange(buf, slot, dev, ssem, rsem):
        return pltpu.make_async_remote_copy(
            src_ref=buf.at[slot], dst_ref=buf.at[slot], send_sem=ssem, recv_sem=rsem.at[slot],
            device_id=dev, device_id_type=MESH,
        )

    for i in range(1, plane_n):
        exchange(plane_sum, me, plane_peer(i)[1], plane_send.at[i], plane_recv).start()

    loads[1].wait()
    for c in range(chunks):
        rows = pl.ds(c * chunk, chunk)
        wide = act[rows, :].astype(F32)
        column = jnp.sum(wide * wide, axis=1, keepdims=True)
        row_sum[z, :, rows] = jnp.broadcast_to(column, (chunk, head)).T[:8]
    for i in range(1, tensor_n):
        exchange(row_sum, z, line_peer(i)[1], row_send.at[i], row_recv).start()

    total = plane_sum[me]
    for i in range(1, plane_n):
        p, dev = plane_peer(i)
        exchange(plane_sum, p, dev, plane_send.at[i], plane_recv).wait_recv()
        total += plane_sum[p]
    line_sum[z] = total
    for i in range(1, tensor_n):
        exchange(line_sum, z, line_peer(i)[1], line_send.at[i], line_recv).start()
    for load in loads[2:]:
        load.wait()
    for i in range(1, tensor_n):
        t, dev = line_peer(i)
        exchange(line_sum, t, dev, line_send.at[i], line_recv).wait_recv()
        total += line_sum[t]
    sumsq = jnp.sum(jnp.sum(total, axis=0, keepdims=True), axis=1, keepdims=True)
    clip = 1.0 / jnp.sqrt(sumsq + 1e-12)

    step_size = STEP_SCALE * width ** (-0.5)

    def updated(s):
        clipped = grad[s].astype(F32) * clip
        rows = pl.ds(s, slab_rows, stride=3)
        moment_new = BETA_ONE * moment[rows, :] + (1.0 - BETA_ONE) * clipped
        variance_new = BETA_TWO * variance[rows, :] + (1.0 - BETA_TWO) * clipped * clipped
        return (master[rows, :] - step_size * moment_new / (jnp.sqrt(variance_new) + 1e-08)).astype(BF16)

    def q_block(t):
        return 3 * (t // 2) + 2 * (t % 2)

    def kv_block(t):
        return 3 * (t // 2) + 1

    def w_slot(r, t, part):
        rows = pl.ds(pl.multiple_of(r * slab_rows, 16), slab_rows)
        column = 2 * q_block(t) + part if part < 2 else 2 * kv_block(t) + t % 2
        return weights.at[column, rows, :]

    owner, my_r = me // hubs, me % hubs

    def to_hub(part):
        return pltpu.make_async_remote_copy(
            src_ref=own.at[part], dst_ref=w_slot(my_r, z, part), send_sem=hub_send.at[part],
            recv_sem=w_recv.at[my_r, z, part], device_id=(g, d, owner), device_id_type=MESH,
        )

    def place(part):
        @pl.when(z == owner)
        def _():
            w_slot(my_r, z, part)[...] = own[part]

        @pl.when(z != owner)
        def _():
            to_hub(part).start()

    for part in range(3):
        own[part] = updated(part)
        place(part)

    square = row_sum[z]
    for i in range(1, tensor_n):
        t, dev = line_peer(i)
        exchange(row_sum, t, dev, row_send.at[i], row_recv).wait_recv()
        square += row_sum[t]
    scale_row = lax.rsqrt(square[:1] * (1.0 / width) + 1e-06)
    for c in range(chunks):
        rows = pl.ds(c * chunk, chunk)
        scale = jnp.broadcast_to(scale_row[:, c * chunk : (c + 1) * chunk], (head, chunk)).T[:, :1]
        normed[rows, :] = (act[rows, :].astype(F32) * scale * gain_ref[z]).astype(BF16)

    def forward(r, t, part, slot, dev):
        return pltpu.make_async_remote_copy(
            src_ref=w_slot(r, t, part), dst_ref=w_slot(r, t, part), send_sem=w_send.at[r, t, part, slot],
            recv_sem=w_recv.at[r, t, part], device_id=dev, device_id_type=MESH,
        )

    def forwards(r, t, part, act_on):
        hub = z * hubs + r
        hub_g, hub_d = hub // dp_n, hub % dp_n
        same_core = core == hub_g % 2
        at_hub = hub == me

        @pl.when(at_hub)
        def _():
            for i in range(1, chip_n):
                act_on(forward(r, t, part, i - 1, (((x + i) % chip_n) * 2 + core, d, z)))

        @pl.when(jnp.logical_and(same_core, d == hub_d))
        def _():
            for i in range(1, dp_n):
                act_on(forward(r, t, part, chip_n - 2 + i, (g, (d + i) % dp_n, z)))

        @pl.when(same_core)
        def _():
            act_on(forward(r, t, part, chip_n + dp_n - 2, (x * 2 + 1 - core, d, z)))

    def start(copy):
        copy.start()

    def wait_send(copy):
        copy.wait_send()

    def chain(buf, b, c, dev_z, ssem, rsem):
        rows = pl.ds(pl.multiple_of(c * piece_rows, 16), piece_rows)
        return pltpu.make_async_remote_copy(
            src_ref=buf.at[b, rows, :], dst_ref=buf.at[b, rows, :], send_sem=ssem.at[b, c], recv_sem=rsem.at[b, c],
            device_id=(g, d, dev_z), device_id_type=MESH,
        )

    def chain_up(b, c):
        return chain(up, b, c, jnp.minimum(z + 1, tensor_n - 1), up_send, up_recv)

    def chain_down(b, c):
        return chain(down, b, c, jnp.maximum(z - 1, 0), down_send, down_recv)

    def span(b):
        pair, j = b // 3, b % 3
        return 2 * pair + j // 2, 2 * pair + (j + 1) // 2

    def multiply(*todo):
        @pl.loop(0, chunks)
        def _(c):
            rows = pl.ds(pl.multiple_of(c * chunk, 16), chunk)
            for b in todo:
                low, high = span(b)
                both = jnp.concatenate([weights[2 * b], weights[2 * b + 1]], axis=1)
                parts[b, rows, :] = jnp.dot(normed[rows, :], both, preferred_element_type=F32)

                @pl.when(jnp.logical_and(z == 0, z < high))
                def _():
                    up[b, rows, :] = parts[b, rows, :].astype(BF16)
                    for half in range(2):
                        chain_up(b, 2 * c + half).start()

                @pl.when(jnp.logical_and(z == tensor_n - 1, z > low))
                def _():
                    down[b, rows, :] = parts[b, rows, :].astype(BF16)
                    for half in range(2):
                        chain_down(b, 2 * c + half).start()

    def slab(j):
        room = jnp.minimum(z, tensor_n - 1 - z)
        near = z + ((j + 1) // 2) * (2 * (j % 2) - 1)
        far = jnp.where(z < tensor_n - 1 - z, j, tensor_n - 1 - j)
        return jnp.where(j <= 2 * room, near, far)

    def rank(t):
        return jnp.where(t > z, 2 * (t - z) - 1, 2 * (z - t))

    def pass_on(t, i):
        r = (d + i) % hubs
        for part in range(3):
            @pl.when(jnp.logical_not(jnp.logical_and(z * hubs + r == me, t == z)))
            def _():
                forward(r, t, part, 0, (g, d, z)).wait_recv()

            forwards(r, t, part, start)

    pass_on(slab(0), 0)

    @pl.loop(0, tensor_n)
    def _(j):
        @pl.when(j + 1 < tensor_n)
        def _():
            pass_on(slab(jnp.minimum(j + 1, tensor_n - 1)), 0)

        t = slab(j)
        for i in range(1, hubs):
            pass_on(t, i)
        complete = rank(t + 1 - 2 * (t % 2)) < rank(t)

        @pl.when(complete)
        def _():
            multiply(kv_block(t), q_block(t))

        @pl.when(jnp.logical_not(complete))
        def _():
            multiply(q_block(t))

    mine = (q_block(z), kv_block(z))
    for slot in range(2):
        final[slot] = parts[mine[slot]]

    def hop(b, c, buf, copy, receives, sends):
        low, high = span(b)
        rows = pl.ds(pl.multiple_of(c * piece_rows, 16), piece_rows)

        @pl.when(receives)
        def _():
            copy(b, c).wait_recv()
            arrived = buf[b, rows, :].astype(F32)

            @pl.when(sends)
            def _():
                buf[b, rows, :] = (parts[b, rows, :] + arrived).astype(BF16)
                copy(b, c).start()

            @pl.when(jnp.logical_and(low <= z, z <= high))
            def _():
                slot = 1 - abs(b % 3 - 1)
                final[slot, rows, :] += arrived

    def hop_up(b, c):
        high = span(b)[1]
        hop(b, c, up, chain_up, jnp.logical_and(z > 0, z <= high), z < high)

    def hop_down(b, c):
        low = span(b)[0]
        hop(b, c, down, chain_down, jnp.logical_and(z < tensor_n - 1, z >= low), z > low)

    early = (blocks - 2) * pieces
    items = blocks * pieces
    lag = 3 * jnp.abs(tensor_n - 1 - 2 * z)
    up_lag = jnp.where(2 * z < tensor_n, 0, lag)
    down_lag = lag - up_lag

    def item(n):
        late = n - early
        b = jnp.where(late < 0, n // pieces, blocks - 2 + late % 2)
        return b, jnp.where(late < 0, n % pieces, late // 2)

    def step(n):
        def one(n, hop_one, mirror):
            @pl.when(jnp.logical_and(n >= 0, n < items))
            def _():
                b, c = item(jnp.clip(n, 0, items - 1))
                hop_one(blocks - 1 - b if mirror else b, c)

        one(n - up_lag, hop_up, False)
        one(n - down_lag, hop_down, True)

    def prepared(raw, gains, rows):
        scaled = raw * lax.rsqrt(jnp.mean(raw * raw, axis=1, keepdims=True) + 1e-06) * gains
        return scaled * cos_ref[rows, :] + pltpu.roll(scaled, head // 2, 1) * sin_ref[rows, :]

    key_gain = key_gain_ref[pl.ds(z // 2, 1), :]
    live = len_ref[0]

    def attend(c):
        rows = pl.ds(c * chunk, chunk)
        seen = (c + 1) * chunk
        keys[rows, :] = prepared(final[1, rows, :head], key_gain, rows).astype(BF16)
        values[rows, :] = final[1, rows, head:].astype(BF16)
        row_pos = lax.broadcasted_iota(jnp.int32, (chunk, seen), 0) + c * chunk
        col_pos = lax.broadcasted_iota(jnp.int32, (chunk, seen), 1)
        allowed = jnp.logical_and(col_pos <= row_pos, col_pos < live)
        for j in range(2):
            raw = final[0, rows, j * head : (j + 1) * head]
            query = (prepared(raw, query_gain_ref[j : j + 1, :], rows) * head ** (-0.5)).astype(BF16)
            scores = lax.dot_general(query, keys[:seen, :], (((1,), (1,)), ((), ())), preferred_element_type=F32)
            scores = jnp.where(allowed, scores, -1e30)
            exps = jnp.exp(scores - jnp.max(scores, axis=1, keepdims=True))
            probs = (exps / jnp.sum(exps, axis=1, keepdims=True)).astype(BF16)
            out_ref[rows, j * head : (j + 1) * head] = jnp.dot(
                probs, values[:seen, :], preferred_element_type=F32
            ).astype(BF16)

    at_end = jnp.logical_or(z == 0, z == tensor_n - 1)

    @pl.when(at_end)
    def _():
        behind = jnp.where(z == 0, down_lag, up_lag)
        for c in range(chunks):
            first = 0 if c == 0 else early + 4 * c + behind

            @pl.loop(first, early + 4 * c + 4 + behind)
            def _(n):
                step(n)

            attend(c)

    @pl.when(jnp.logical_not(at_end))
    def _():
        @pl.loop(0, items + lag)
        def _(n):
            step(n)

        for c in range(chunks):
            attend(c)

    for i in range(1, plane_n):
        exchange(plane_sum, me, plane_peer(i)[1], plane_send.at[i], plane_recv).wait_send()
    for i in range(1, tensor_n):
        dev = line_peer(i)[1]
        exchange(line_sum, z, dev, line_send.at[i], line_recv).wait_send()
        exchange(row_sum, z, dev, row_send.at[i], row_recv).wait_send()

    @pl.when(z != owner)
    def _():
        for part in range(3):
            to_hub(part).wait_send()

    @pl.loop(0, tensor_n)
    def _(t):
        for r in range(hubs):
            for part in range(3):
                forwards(r, t, part, wait_send)

    @pl.loop(0, blocks)
    def _(b):
        low, high = span(b)

        @pl.loop(0, pieces)
        def _(c):
            @pl.when(z < high)
            def _():
                chain_up(b, c).wait_send()

            @pl.when(z > low)
            def _():
                chain_down(b, c).wait_send()


def shards(sizes, activations, norm_gain, master_weight, grad, moment, variance, query_gain, key_gain, prompt_len):
    group_n, dp_n, tensor_n = sizes
    plane_n = group_n * dp_n
    hubs = plane_n // tensor_n
    width = norm_gain.shape[0]
    length, feat = activations.shape
    slab_rows, _, slots, head = master_weight.shape
    pair = 2 * head
    blocks = 3 * tensor_n // 2
    chunk = 256 if length % 256 == 0 else length
    pieces = 2 * (length // chunk)
    cosine, sine = rope_tables(length, head)

    def flat(array):
        return array.reshape(slab_rows * slots, head)

    hbm = pl.BlockSpec(memory_space=pl.ANY)
    vmem = pl.BlockSpec(memory_space=pltpu.VMEM)
    dma = pltpu.SemaphoreType.DMA
    return pl.pallas_call(
        functools.partial(kernel, (group_n, dp_n, tensor_n, width)),
        out_shape=jax.ShapeDtypeStruct((length, pair), BF16),
        in_specs=[hbm, vmem, hbm, hbm, hbm, hbm, vmem, vmem, vmem, vmem, pl.BlockSpec(memory_space=pltpu.SMEM)],
        out_specs=vmem,
        scratch_shapes=[
            pltpu.VMEM((length, feat), BF16),
            pltpu.VMEM((length, feat), BF16),
            pltpu.VMEM((slab_rows * slots, head), F32),
            pltpu.VMEM((slots, slab_rows, head), BF16),
            pltpu.VMEM((slab_rows * slots, head), F32),
            pltpu.VMEM((slab_rows * slots, head), F32),
            pltpu.VMEM((slots, slab_rows, head), BF16),
            pltpu.VMEM((2 * blocks, feat, head), BF16),
            pltpu.VMEM((blocks, length, pair), F32),
            pltpu.VMEM((blocks, length, pair), BF16),
            pltpu.VMEM((blocks, length, pair), BF16),
            pltpu.VMEM((2, length, pair), F32),
            pltpu.VMEM((length, head), BF16),
            pltpu.VMEM((length, head), BF16),
            pltpu.VMEM((plane_n, 8, head), F32),
            pltpu.VMEM((tensor_n, 8, head), F32),
            pltpu.VMEM((tensor_n, 8, length), F32),
            dma((5,)),
            dma((plane_n,)),
            dma((plane_n,)),
            dma((tensor_n,)),
            dma((tensor_n,)),
            dma((tensor_n,)),
            dma((tensor_n,)),
            dma((3,)),
            dma((hubs, tensor_n, 3)),
            dma((hubs, tensor_n, 3, group_n // 2 + dp_n - 1)),
            dma((blocks, pieces)),
            dma((blocks, pieces)),
            dma((blocks, pieces)),
            dma((blocks, pieces)),
        ],
        compiler_params=pltpu.CompilerParams(
            collective_id=0, has_side_effects=True, vmem_limit_bytes=60 * 1024 * 1024
        ),
        name="step_and_prefill",
    )(
        activations,
        norm_gain.reshape(tensor_n, 1, feat),
        flat(master_weight),
        jnp.transpose(grad.reshape(slab_rows, slots, head), (1, 0, 2)),
        flat(moment),
        flat(variance),
        query_gain,
        key_gain,
        cosine,
        sine,
        prompt_len,
    )


def solution(mesh):
    in_specs = (
        P(("group", "dp"), "tensor"),
        P(),
        P(("group", "dp"), "tensor", None, None),
        P(("group", "dp"), "tensor", None, None),
        P(("group", "dp"), "tensor", None, None),
        P(("group", "dp"), "tensor", None, None),
        P("tensor", None),
        P(),
        P(("group", "dp")),
    )
    out_specs = P(("group", "dp"), "tensor")
    sizes = tuple(mesh.shape[axis] for axis in ("group", "dp", "tensor"))
    return jax.shard_map(
        functools.partial(shards, sizes), mesh=mesh, in_specs=in_specs, out_specs=out_specs, check_vma=False
    )
```

```python
import functools

import jax
import jax.numpy as jnp
import numpy as np
from jax import lax
from jax.experimental import pallas as pl
from jax.experimental.pallas import tpu as pltpu
from jax.sharding import PartitionSpec as P

STEP_SCALE = 0.5
BETA_ONE = 0.9
BETA_TWO = 0.95
ROPE_BASE = 500000.0
MESH = pl.DeviceIdType.MESH
BF16 = jnp.bfloat16
F32 = jnp.float32


def rope_tables(length, head_size):
    positions = np.arange(length, dtype=np.float32)
    exponent = np.arange(head_size // 2, dtype=np.float32) * np.float32(2.0) / np.float32(head_size)
    inverse = np.power(np.float32(ROPE_BASE), -exponent).astype(np.float32)
    angles = (positions[:, None] * inverse[None, :]).astype(np.float32)
    cosine, sine = np.cos(angles), np.sin(angles)
    return (
        np.concatenate([cosine, cosine], axis=1).astype(np.float32),
        np.concatenate([-sine, sine], axis=1).astype(np.float32),
    )


def kernel(
    sizes,
    act_hbm, gain_ref, master_hbm, grad_hbm, moment_hbm, variance_hbm, query_gain_ref, key_gain_ref,
    cos_ref, sin_ref, len_ref,
    out_ref,
    act, normed, master, grad, moment, variance, own, weights, parts, up, down, final, keys, values,
    plane_sum, line_sum, row_sum,
    in_sem, plane_send, plane_recv, line_send, line_recv, row_send, row_recv,
    hub_send, w_recv, w_send, up_send, up_recv, down_send, down_recv,
):
    group_n, dp_n, tensor_n, width = sizes
    plane_n = group_n * dp_n
    chip_n = group_n // 2
    hubs = plane_n // tensor_n
    length, feat = act.shape
    slab_rows = grad.shape[1]
    head = 128
    chunk = 256 if length % 256 == 0 else length
    chunks = length // chunk

    g = lax.axis_index("group")
    d = lax.axis_index("dp")
    z = lax.axis_index("tensor")
    me = g * dp_n + d
    x, core = g // 2, g % 2

    def plane_peer(i):
        p = (me + i) % plane_n
        return p, (p // dp_n, p % dp_n, z)

    def line_peer(i):
        t = (z + i) % tensor_n
        return t, (g, d, t)

    loads = [
        pltpu.make_async_copy(src, dst, in_sem.at[i])
        for i, (src, dst) in enumerate(
            [(grad_hbm, grad), (act_hbm, act), (moment_hbm, moment), (variance_hbm, variance), (master_hbm, master)]
        )
    ]
    for load in loads:
        load.start()

    barrier = pltpu.get_barrier_semaphore()
    for i in range(1, plane_n):
        pl.semaphore_signal(barrier, inc=1, device_id=plane_peer(i)[1], device_id_type=MESH)
    for i in range(1, tensor_n):
        pl.semaphore_signal(barrier, inc=1, device_id=line_peer(i)[1], device_id_type=MESH)

    loads[0].wait()
    tile = jnp.zeros((8, head), F32)
    for s in range(3):
        piece = grad[s].astype(F32)
        tile += jnp.sum((piece * piece).reshape(slab_rows // 8, 8, head), axis=0)
    plane_sum[me] = tile
    pl.semaphore_wait(barrier, plane_n + tensor_n - 2)

    def exchange(buf, slot, dev, ssem, rsem):
        return pltpu.make_async_remote_copy(
            src_ref=buf.at[slot], dst_ref=buf.at[slot], send_sem=ssem, recv_sem=rsem.at[slot],
            device_id=dev, device_id_type=MESH,
        )

    for i in range(1, plane_n):
        exchange(plane_sum, me, plane_peer(i)[1], plane_send.at[i], plane_recv).start()

    loads[1].wait()
    for c in range(chunks):
        rows = pl.ds(c * chunk, chunk)
        wide = act[rows, :].astype(F32)
        column = jnp.sum(wide * wide, axis=1, keepdims=True)
        row_sum[z, :, rows] = jnp.broadcast_to(column, (chunk, head)).T[:8]
    for i in range(1, tensor_n):
        exchange(row_sum, z, line_peer(i)[1], row_send.at[i], row_recv).start()

    total = plane_sum[me]
    for i in range(1, plane_n):
        p, dev = plane_peer(i)
        exchange(plane_sum, p, dev, plane_send.at[i], plane_recv).wait_recv()
        total += plane_sum[p]
    line_sum[z] = total
    for i in range(1, tensor_n):
        exchange(line_sum, z, line_peer(i)[1], line_send.at[i], line_recv).start()
    for load in loads[2:]:
        load.wait()
    for i in range(1, tensor_n):
        t, dev = line_peer(i)
        exchange(line_sum, t, dev, line_send.at[i], line_recv).wait_recv()
        total += line_sum[t]
    sumsq = jnp.sum(jnp.sum(total, axis=0, keepdims=True), axis=1, keepdims=True)
    clip = 1.0 / jnp.sqrt(sumsq + 1e-12)

    step_size = STEP_SCALE * width ** (-0.5)

    def updated(s):
        clipped = grad[s].astype(F32) * clip
        rows = pl.ds(s, slab_rows, stride=3)
        moment_new = BETA_ONE * moment[rows, :] + (1.0 - BETA_ONE) * clipped
        variance_new = BETA_TWO * variance[rows, :] + (1.0 - BETA_TWO) * clipped * clipped
        return (master[rows, :] - step_size * moment_new / (jnp.sqrt(variance_new) + 1e-08)).astype(BF16)

    def w_slot(r, t, part):
        rows = pl.ds(pl.multiple_of(r * slab_rows, 16), slab_rows)
        return weights.at[3 * t + part, rows, :]

    owner, my_r = me // hubs, me % hubs

    def to_hub(part):
        return pltpu.make_async_remote_copy(
            src_ref=own.at[part], dst_ref=w_slot(my_r, z, part), send_sem=hub_send.at[part],
            recv_sem=w_recv.at[my_r, z, part], device_id=(g, d, owner), device_id_type=MESH,
        )

    def place(part):
        @pl.when(z == owner)
        def _():
            w_slot(my_r, z, part)[...] = own[part]

        @pl.when(z != owner)
        def _():
            to_hub(part).start()

    for part in range(3):
        own[part] = updated(part)
        place(part)

    square = row_sum[z]
    for i in range(1, tensor_n):
        t, dev = line_peer(i)
        exchange(row_sum, t, dev, row_send.at[i], row_recv).wait_recv()
        square += row_sum[t]
    scale_row = lax.rsqrt(square[:1] * (1.0 / width) + 1e-06)
    for c in range(chunks):
        rows = pl.ds(c * chunk, chunk)
        scale = jnp.broadcast_to(scale_row[:, c * chunk : (c + 1) * chunk], (head, chunk)).T[:, :1]
        normed[rows, :] = (act[rows, :].astype(F32) * scale * gain_ref[z]).astype(BF16)

    def forward(r, t, part, slot, dev):
        return pltpu.make_async_remote_copy(
            src_ref=w_slot(r, t, part), dst_ref=w_slot(r, t, part), send_sem=w_send.at[r, t, part, slot],
            recv_sem=w_recv.at[r, t, part], device_id=dev, device_id_type=MESH,
        )

    def forwards(r, t, part, act_on):
        hub = z * hubs + r
        hub_g, hub_d = hub // dp_n, hub % dp_n
        same_core = core == hub_g % 2
        at_hub = hub == me

        @pl.when(at_hub)
        def _():
            for i in range(1, chip_n):
                act_on(forward(r, t, part, i - 1, (((x + i) % chip_n) * 2 + core, d, z)))

        @pl.when(jnp.logical_and(same_core, d == hub_d))
        def _():
            for i in range(1, dp_n):
                act_on(forward(r, t, part, chip_n - 2 + i, (g, (d + i) % dp_n, z)))

        @pl.when(same_core)
        def _():
            act_on(forward(r, t, part, chip_n + dp_n - 2, (x * 2 + 1 - core, d, z)))

    def start(copy):
        copy.start()

    def wait_send(copy):
        copy.wait_send()

    def chain(buf, column, c, dev_z, ssem, rsem):
        rows = pl.ds(pl.multiple_of(c * chunk, 16), chunk)
        return pltpu.make_async_remote_copy(
            src_ref=buf.at[column, rows, :], dst_ref=buf.at[column, rows, :], send_sem=ssem.at[column, c],
            recv_sem=rsem.at[column, c], device_id=(g, d, dev_z), device_id_type=MESH,
        )

    def chain_up(column, c):
        return chain(up, column, c, jnp.minimum(z + 1, tensor_n - 1), up_send, up_recv)

    def chain_down(column, c):
        return chain(down, column, c, jnp.maximum(z - 1, 0), down_send, down_recv)

    def span(t, part):
        first = t if part < 2 else 2 * (t // 2)
        return first, first if part < 2 else first + 1

    def multiply(t):
        @pl.loop(0, chunks)
        def _(c):
            rows = pl.ds(pl.multiple_of(c * chunk, 16), chunk)
            both = jnp.concatenate([weights[3 * t], weights[3 * t + 1]], axis=1)
            product = jnp.dot(normed[rows, :], both, preferred_element_type=F32)
            parts[3 * t, rows, :] = product[:, :head]
            parts[3 * t + 1, rows, :] = product[:, head:]
            parts[3 * t + 2, rows, :] = jnp.dot(normed[rows, :], weights[3 * t + 2], preferred_element_type=F32)

            def begin(buf, copy, next_to):
                for part in range(3):
                    buf[3 * t + part, rows, :] = parts[3 * t + part, rows, :].astype(BF16)
                    if part == 2:
                        copy(3 * t + part, c).start()
                    else:
                        @pl.when(jnp.logical_and(t != z, t != next_to))
                        def _():
                            copy(3 * t + part, c).start()

            @pl.when(z == 0)
            def _():
                begin(up, chain_up, 1)

            @pl.when(z == tensor_n - 1)
            def _():
                begin(down, chain_down, tensor_n - 2)

    def slab(j):
        room = jnp.minimum(z, tensor_n - 1 - z)
        near = z + ((j + 1) // 2) * (2 * (j % 2) - 1)
        far = jnp.where(z < tensor_n - 1 - z, j, tensor_n - 1 - j)
        return jnp.where(j <= 2 * room, near, far)

    def pass_on(t, i):
        r = (d + i) % hubs
        for part in range(3):
            @pl.when(jnp.logical_not(jnp.logical_and(z * hubs + r == me, t == z)))
            def _():
                forward(r, t, part, 0, (g, d, z)).wait_recv()

            forwards(r, t, part, start)

    pass_on(slab(0), 0)

    @pl.loop(0, tensor_n)
    def _(j):
        @pl.when(j + 1 < tensor_n)
        def _():
            pass_on(slab(jnp.minimum(j + 1, tensor_n - 1)), 0)

        t = slab(j)
        for i in range(1, hubs):
            pass_on(t, i)
        multiply(t)

    @pl.when(z == 0)
    def _():
        for c in range(chunks):
            for part in range(2):
                chain_up(3 + part, c).start()

    @pl.when(z == tensor_n - 1)
    def _():
        for c in range(chunks):
            for part in range(2):
                chain_down(3 * (tensor_n - 2) + part, c).start()

    pair = 2 * (z // 2)
    final[0] = parts[3 * z]
    final[1] = parts[3 * z + 1]
    final[2] = parts[3 * pair + 2]
    final[3] = parts[3 * pair + 5]

    def hop(t, part, c, buf, copy, receives, sends):
        low, high = span(t, part)
        rows = pl.ds(pl.multiple_of(c * chunk, 16), chunk)
        column = 3 * t + part

        @pl.when(receives)
        def _():
            copy(column, c).wait_recv()
            arrived = buf[column, rows, :].astype(F32)

            @pl.when(sends)
            def _():
                buf[column, rows, :] = (parts[column, rows, :] + arrived).astype(BF16)
                copy(column, c).start()

            @pl.when(jnp.logical_and(low <= z, z <= high))
            def _():
                slot = part if part < 2 else 2 + t % 2
                final[slot, rows, :] += arrived

    def hop_up(t, part, c):
        high = span(t, part)[1]
        hop(t, part, c, up, chain_up, jnp.logical_and(z > 0, z <= high), z < high)

    def hop_down(t, part, c):
        low = span(t, part)[0]
        hop(t, part, c, down, chain_down, jnp.logical_and(z < tensor_n - 1, z >= low), z > low)

    rounds = tensor_n * chunks
    lag = jnp.abs(tensor_n - 1 - 2 * z)
    up_lag = jnp.where(2 * z < tensor_n, 0, lag)
    down_lag = lag - up_lag

    def turn(n):
        def one(n, hop_one, mirror):
            slab_of = jnp.clip(n, 0, rounds - 1) // chunks
            t = tensor_n - 1 - slab_of if mirror else slab_of
            late = n >= rounds
            c = jnp.where(late, n - rounds, n % chunks)
            t = jnp.where(late, tensor_n - 2 if mirror else 1, t)

            @pl.when(jnp.logical_and(n >= 0, n < rounds + chunks))
            def _():
                @pl.when(jnp.logical_or(late, slab_of != 1))
                def _():
                    hop_one(t, 0, c)
                    hop_one(t, 1, c)

                @pl.when(jnp.logical_not(late))
                def _():
                    hop_one(t, 2, c)

        one(n - up_lag, hop_up, False)
        one(n - down_lag, hop_down, True)

    def prepared(raw, gains, rows):
        scaled = raw * lax.rsqrt(jnp.mean(raw * raw, axis=1, keepdims=True) + 1e-06) * gains
        return scaled * cos_ref[rows, :] + pltpu.roll(scaled, head // 2, 1) * sin_ref[rows, :]

    key_gain = key_gain_ref[pl.ds(z // 2, 1), :]
    live = len_ref[0]

    def attend(c):
        rows = pl.ds(c * chunk, chunk)
        seen = (c + 1) * chunk
        keys[rows, :] = prepared(final[2, rows, :], key_gain, rows).astype(BF16)
        values[rows, :] = final[3, rows, :].astype(BF16)
        row_pos = lax.broadcasted_iota(jnp.int32, (chunk, seen), 0) + c * chunk
        col_pos = lax.broadcasted_iota(jnp.int32, (chunk, seen), 1)
        allowed = jnp.logical_and(col_pos <= row_pos, col_pos < live)
        for j in range(2):
            raw = final[j, rows, :]
            query = (prepared(raw, query_gain_ref[j : j + 1, :], rows) * head ** (-0.5)).astype(BF16)
            scores = lax.dot_general(query, keys[:seen, :], (((1,), (1,)), ((), ())), preferred_element_type=F32)
            scores = jnp.where(allowed, scores, -1e30)
            exps = jnp.exp(scores - jnp.max(scores, axis=1, keepdims=True))
            probs = (exps / jnp.sum(exps, axis=1, keepdims=True)).astype(BF16)
            out_ref[rows, j * head : (j + 1) * head] = jnp.dot(
                probs, values[:seen, :], preferred_element_type=F32
            ).astype(BF16)

    at_end = jnp.logical_or(z == 0, z == tensor_n - 1)
    next_to = jnp.logical_or(z == 1, z == tensor_n - 2)

    def stop(c):
        end = rounds - chunks + c + 1 + lag
        beside = rounds + jnp.maximum(c + 1, lag)
        return jnp.where(at_end, end, jnp.where(next_to, beside, rounds + chunks + lag))

    for c in range(chunks):
        @pl.loop(0 if c == 0 else stop(c - 1), stop(c))
        def _(n):
            turn(n)

        attend(c)

    for i in range(1, plane_n):
        exchange(plane_sum, me, plane_peer(i)[1], plane_send.at[i], plane_recv).wait_send()
    for i in range(1, tensor_n):
        dev = line_peer(i)[1]
        exchange(line_sum, z, dev, line_send.at[i], line_recv).wait_send()
        exchange(row_sum, z, dev, row_send.at[i], row_recv).wait_send()

    @pl.when(z != owner)
    def _():
        for part in range(3):
            to_hub(part).wait_send()

    @pl.loop(0, tensor_n)
    def _(t):
        for r in range(hubs):
            for part in range(3):
                forwards(r, t, part, wait_send)

    @pl.loop(0, tensor_n)
    def _(t):
        for part in range(3):
            low, high = span(t, part)

            @pl.loop(0, chunks)
            def _(c):
                @pl.when(z < high)
                def _():
                    chain_up(3 * t + part, c).wait_send()

                @pl.when(z > low)
                def _():
                    chain_down(3 * t + part, c).wait_send()


def shards(sizes, activations, norm_gain, master_weight, grad, moment, variance, query_gain, key_gain, prompt_len):
    group_n, dp_n, tensor_n = sizes
    plane_n = group_n * dp_n
    hubs = plane_n // tensor_n
    width = norm_gain.shape[0]
    length, feat = activations.shape
    slab_rows, _, slots, head = master_weight.shape
    pair = 2 * head
    columns = 3 * tensor_n
    chunk = 256 if length % 256 == 0 else length
    chunks = length // chunk
    cosine, sine = rope_tables(length, head)

    def flat(array):
        return array.reshape(slab_rows * slots, head)

    hbm = pl.BlockSpec(memory_space=pl.ANY)
    vmem = pl.BlockSpec(memory_space=pltpu.VMEM)
    dma = pltpu.SemaphoreType.DMA
    return pl.pallas_call(
        functools.partial(kernel, (group_n, dp_n, tensor_n, width)),
        out_shape=jax.ShapeDtypeStruct((length, pair), BF16),
        in_specs=[hbm, vmem, hbm, hbm, hbm, hbm, vmem, vmem, vmem, vmem, pl.BlockSpec(memory_space=pltpu.SMEM)],
        out_specs=vmem,
        scratch_shapes=[
            pltpu.VMEM((length, feat), BF16),
            pltpu.VMEM((length, feat), BF16),
            pltpu.VMEM((slab_rows * slots, head), F32),
            pltpu.VMEM((slots, slab_rows, head), BF16),
            pltpu.VMEM((slab_rows * slots, head), F32),
            pltpu.VMEM((slab_rows * slots, head), F32),
            pltpu.VMEM((slots, slab_rows, head), BF16),
            pltpu.VMEM((columns, feat, head), BF16),
            pltpu.VMEM((columns, length, head), F32),
            pltpu.VMEM((columns, length, head), BF16),
            pltpu.VMEM((columns, length, head), BF16),
            pltpu.VMEM((4, length, head), F32),
            pltpu.VMEM((length, head), BF16),
            pltpu.VMEM((length, head), BF16),
            pltpu.VMEM((plane_n, 8, head), F32),
            pltpu.VMEM((tensor_n, 8, head), F32),
            pltpu.VMEM((tensor_n, 8, length), F32),
            dma((5,)),
            dma((plane_n,)),
            dma((plane_n,)),
            dma((tensor_n,)),
            dma((tensor_n,)),
            dma((tensor_n,)),
            dma((tensor_n,)),
            dma((3,)),
            dma((hubs, tensor_n, 3)),
            dma((hubs, tensor_n, 3, group_n // 2 + dp_n - 1)),
            dma((columns, chunks)),
            dma((columns, chunks)),
            dma((columns, chunks)),
            dma((columns, chunks)),
        ],
        compiler_params=pltpu.CompilerParams(
            collective_id=0, has_side_effects=True, vmem_limit_bytes=60 * 1024 * 1024
        ),
        name="step_and_prefill",
    )(
        activations,
        norm_gain.reshape(tensor_n, 1, feat),
        flat(master_weight),
        jnp.transpose(grad.reshape(slab_rows, slots, head), (1, 0, 2)),
        flat(moment),
        flat(variance),
        query_gain,
        key_gain,
        cosine,
        sine,
        prompt_len,
    )


def solution(mesh):
    in_specs = (
        P(("group", "dp"), "tensor"),
        P(),
        P(("group", "dp"), "tensor", None, None),
        P(("group", "dp"), "tensor", None, None),
        P(("group", "dp"), "tensor", None, None),
        P(("group", "dp"), "tensor", None, None),
        P("tensor", None),
        P(),
        P(("group", "dp")),
    )
    out_specs = P(("group", "dp"), "tensor")
    sizes = tuple(mesh.shape[axis] for axis in ("group", "dp", "tensor"))
    return jax.shard_map(
        functools.partial(shards, sizes), mesh=mesh, in_specs=in_specs, out_specs=out_specs, check_vma=False
    )
```

```python
import functools

import jax
import jax.numpy as jnp
import numpy as np
from jax import lax
from jax.experimental import pallas as pl
from jax.experimental.pallas import tpu as pltpu
from jax.sharding import PartitionSpec as P

STEP_SCALE = 0.5
BETA_ONE = 0.9
BETA_TWO = 0.95
ROPE_BASE = 500000.0
MESH = pl.DeviceIdType.MESH
BF16 = jnp.bfloat16
F32 = jnp.float32


def rope_tables(length, head_size):
    positions = np.arange(length, dtype=np.float32)
    exponent = np.arange(head_size // 2, dtype=np.float32) * np.float32(2.0) / np.float32(head_size)
    inverse = np.power(np.float32(ROPE_BASE), -exponent).astype(np.float32)
    angles = (positions[:, None] * inverse[None, :]).astype(np.float32)
    cosine, sine = np.cos(angles), np.sin(angles)
    return (
        np.concatenate([cosine, cosine], axis=1).astype(np.float32),
        np.concatenate([-sine, sine], axis=1).astype(np.float32),
    )


def kernel(
    sizes,
    act_hbm, gain_ref, master_hbm, grad_hbm, moment_hbm, variance_hbm, query_gain_ref, key_gain_ref,
    cos_ref, sin_ref, len_ref,
    out_ref,
    act, normed, master, grad, moment, variance, own, weights, parts, up, down, final, keys, values,
    plane_sum, line_sum, row_sum,
    in_sem, plane_send, plane_recv, line_send, line_recv, row_send, row_recv,
    hub_send, w_recv, w_send, up_send, up_recv, down_send, down_recv,
):
    group_n, dp_n, tensor_n, width = sizes
    plane_n = group_n * dp_n
    chip_n = group_n // 2
    hubs = plane_n // tensor_n
    length, feat = act.shape
    slab_rows = grad.shape[1]
    head = 128
    chunk = 256 if length % 256 == 0 else length
    chunks = length // chunk

    g = lax.axis_index("group")
    d = lax.axis_index("dp")
    z = lax.axis_index("tensor")
    me = g * dp_n + d
    x, core = g // 2, g % 2

    def plane_peer(i):
        p = (me + i) % plane_n
        return p, (p // dp_n, p % dp_n, z)

    def line_peer(i):
        t = (z + i) % tensor_n
        return t, (g, d, t)

    loads = [
        pltpu.make_async_copy(src, dst, in_sem.at[i])
        for i, (src, dst) in enumerate(
            [(grad_hbm, grad), (act_hbm, act), (moment_hbm, moment), (variance_hbm, variance), (master_hbm, master)]
        )
    ]
    for load in loads:
        load.start()

    barrier = pltpu.get_barrier_semaphore()
    for i in range(1, plane_n):
        pl.semaphore_signal(barrier, inc=1, device_id=plane_peer(i)[1], device_id_type=MESH)
    for i in range(1, tensor_n):
        pl.semaphore_signal(barrier, inc=1, device_id=line_peer(i)[1], device_id_type=MESH)
    for h in range(1, chip_n):
        for i in range(1, tensor_n):
            beside = (((x + h) % chip_n) * 2 + core, d, (z + i) % tensor_n)
            pl.semaphore_signal(barrier, inc=1, device_id=beside, device_id_type=MESH)

    loads[0].wait()
    tile = jnp.zeros((8, head), F32)
    for s in range(3):
        piece = grad[s].astype(F32)
        tile += jnp.sum((piece * piece).reshape(slab_rows // 8, 8, head), axis=0)
    plane_sum[me] = tile
    pl.semaphore_wait(barrier, plane_n - 1 + chip_n * (tensor_n - 1))

    def exchange(buf, slot, dev, ssem, rsem):
        return pltpu.make_async_remote_copy(
            src_ref=buf.at[slot], dst_ref=buf.at[slot], send_sem=ssem, recv_sem=rsem.at[slot],
            device_id=dev, device_id_type=MESH,
        )

    for i in range(1, plane_n):
        exchange(plane_sum, me, plane_peer(i)[1], plane_send.at[i], plane_recv).start()

    loads[1].wait()
    for c in range(chunks):
        rows = pl.ds(c * chunk, chunk)
        wide = act[rows, :].astype(F32)
        column = jnp.sum(wide * wide, axis=1, keepdims=True)
        row_sum[z, :, rows] = jnp.broadcast_to(column, (chunk, head)).T[:8]
    for i in range(1, tensor_n):
        exchange(row_sum, z, line_peer(i)[1], row_send.at[i], row_recv).start()

    total = plane_sum[me]
    for i in range(1, plane_n):
        p, dev = plane_peer(i)
        exchange(plane_sum, p, dev, plane_send.at[i], plane_recv).wait_recv()
        total += plane_sum[p]
    line_sum[z] = total
    for i in range(1, tensor_n):
        exchange(line_sum, z, line_peer(i)[1], line_send.at[i], line_recv).start()
    for load in loads[2:]:
        load.wait()
    for i in range(1, tensor_n):
        t, dev = line_peer(i)
        exchange(line_sum, t, dev, line_send.at[i], line_recv).wait_recv()
        total += line_sum[t]
    sumsq = jnp.sum(jnp.sum(total, axis=0, keepdims=True), axis=1, keepdims=True)
    clip = 1.0 / jnp.sqrt(sumsq + 1e-12)

    step_size = STEP_SCALE * width ** (-0.5)

    def updated(s):
        clipped = grad[s].astype(F32) * clip
        rows = pl.ds(s, slab_rows, stride=3)
        moment_new = BETA_ONE * moment[rows, :] + (1.0 - BETA_ONE) * clipped
        variance_new = BETA_TWO * variance[rows, :] + (1.0 - BETA_TWO) * clipped * clipped
        return (master[rows, :] - step_size * moment_new / (jnp.sqrt(variance_new) + 1e-08)).astype(BF16)

    share = slab_rows // chip_n

    def w_slot(r, h, t, part):
        rows = pl.ds(pl.multiple_of(r * slab_rows + h * share, 16), share)
        return weights.at[3 * t + part, rows, :]

    owner, my_r = me // hubs, me % hubs

    def to_hub(h, part):
        return pltpu.make_async_remote_copy(
            src_ref=own.at[part, h * share : (h + 1) * share, :], dst_ref=w_slot(my_r, h, z, part),
            send_sem=hub_send.at[h, part], recv_sem=w_recv.at[my_r * chip_n + h, z, part],
            device_id=(((x + h) % chip_n) * 2 + core, d, owner), device_id_type=MESH,
        )

    for part in range(3):
        own[part] = updated(part)

        @pl.when(z == owner)
        def _():
            w_slot(my_r, 0, z, part)[...] = own[part, :share]

        @pl.when(z != owner)
        def _():
            to_hub(0, part).start()

        for h in range(1, chip_n):
            to_hub(h, part).start()

    square = row_sum[z]
    for i in range(1, tensor_n):
        t, dev = line_peer(i)
        exchange(row_sum, t, dev, row_send.at[i], row_recv).wait_recv()
        square += row_sum[t]
    scale_row = lax.rsqrt(square[:1] * (1.0 / width) + 1e-06)
    for c in range(chunks):
        rows = pl.ds(c * chunk, chunk)
        scale = jnp.broadcast_to(scale_row[:, c * chunk : (c + 1) * chunk], (head, chunk)).T[:, :1]
        normed[rows, :] = (act[rows, :].astype(F32) * scale * gain_ref[z]).astype(BF16)

    def forward(r, h, t, part, slot, dev):
        return pltpu.make_async_remote_copy(
            src_ref=w_slot(r, h, t, part), dst_ref=w_slot(r, h, t, part),
            send_sem=w_send.at[r * chip_n + h, t, part, slot], recv_sem=w_recv.at[r * chip_n + h, t, part],
            device_id=dev, device_id_type=MESH,
        )

    def origin(r):
        hub_g = (z * hubs + r) // dp_n
        return hub_g // 2, hub_g % 2, (z * hubs + r) % dp_n

    def forwards(r, h, t, part, act_on):
        from_x, from_core, from_d = origin(r)
        same_core = core == from_core
        same_line = jnp.logical_and(same_core, d == from_d)

        @pl.when(jnp.logical_and(same_line, x == (from_x + h) % chip_n))
        def _():
            for i in range(1, chip_n):
                act_on(forward(r, h, t, part, i - 1, (((x + i) % chip_n) * 2 + core, d, z)))

        @pl.when(same_line)
        def _():
            for i in range(1, dp_n):
                act_on(forward(r, h, t, part, chip_n - 2 + i, (g, (d + i) % dp_n, z)))

        @pl.when(same_core)
        def _():
            act_on(forward(r, h, t, part, chip_n + dp_n - 2, (x * 2 + 1 - core, d, z)))

    def start(copy):
        copy.start()

    def wait_send(copy):
        copy.wait_send()

    def chain(buf, column, c, dev_z, ssem, rsem):
        rows = pl.ds(pl.multiple_of(c * chunk, 16), chunk)
        return pltpu.make_async_remote_copy(
            src_ref=buf.at[column, rows, :], dst_ref=buf.at[column, rows, :], send_sem=ssem.at[column, c],
            recv_sem=rsem.at[column, c], device_id=(g, d, dev_z), device_id_type=MESH,
        )

    def chain_up(column, c):
        return chain(up, column, c, jnp.minimum(z + 1, tensor_n - 1), up_send, up_recv)

    def chain_down(column, c):
        return chain(down, column, c, jnp.maximum(z - 1, 0), down_send, down_recv)

    def span(t, part):
        first = t if part < 2 else 2 * (t // 2)
        return first, first if part < 2 else first + 1

    def multiply(t):
        @pl.loop(0, chunks)
        def _(c):
            rows = pl.ds(pl.multiple_of(c * chunk, 16), chunk)
            both = jnp.concatenate([weights[3 * t], weights[3 * t + 1]], axis=1)
            product = jnp.dot(normed[rows, :], both, preferred_element_type=F32)
            parts[3 * t, rows, :] = product[:, :head]
            parts[3 * t + 1, rows, :] = product[:, head:]
            parts[3 * t + 2, rows, :] = jnp.dot(normed[rows, :], weights[3 * t + 2], preferred_element_type=F32)

            def begin(buf, copy, next_to):
                for part in range(3):
                    buf[3 * t + part, rows, :] = parts[3 * t + part, rows, :].astype(BF16)
                    if part == 2:
                        copy(3 * t + part, c).start()
                    else:
                        @pl.when(jnp.logical_and(t != z, t != next_to))
                        def _():
                            copy(3 * t + part, c).start()

            @pl.when(z == 0)
            def _():
                begin(up, chain_up, 1)

            @pl.when(z == tensor_n - 1)
            def _():
                begin(down, chain_down, tensor_n - 2)

    def slab(j):
        room = jnp.minimum(z, tensor_n - 1 - z)
        near = z + ((j + 1) // 2) * (2 * (j % 2) - 1)
        far = jnp.where(z < tensor_n - 1 - z, j, tensor_n - 1 - j)
        return jnp.where(j <= 2 * room, near, far)

    def pass_on(t, i, q):
        r = (d + i) % hubs
        h = (x - origin(r)[0] + chip_n + q) % chip_n
        for part in range(3):
            @pl.when(jnp.logical_not(jnp.logical_and(z * hubs + r == me, jnp.logical_and(t == z, h == 0))))
            def _():
                forward(r, h, t, part, 0, (g, d, z)).wait_recv()

            forwards(r, h, t, part, start)

    @pl.loop(-2, tensor_n)
    def _(j):
        @pl.when(j + 2 < tensor_n)
        def _():
            pass_on(slab(jnp.minimum(j + 2, tensor_n - 1)), 0, 0)

        @pl.when(jnp.logical_and(j + 1 >= 0, j + 1 < tensor_n))
        def _():
            t = slab(jnp.clip(j + 1, 0, tensor_n - 1))
            for q in range(1, chip_n):
                pass_on(t, 0, q)

        @pl.when(j >= 0)
        def _():
            t = slab(jnp.maximum(j, 0))
            for i in range(1, hubs):
                for q in range(chip_n):
                    pass_on(t, i, q)
            multiply(t)

    @pl.when(z == 0)
    def _():
        for c in range(chunks):
            for part in range(2):
                chain_up(3 + part, c).start()

    @pl.when(z == tensor_n - 1)
    def _():
        for c in range(chunks):
            for part in range(2):
                chain_down(3 * (tensor_n - 2) + part, c).start()

    pair = 2 * (z // 2)
    final[0] = parts[3 * z]
    final[1] = parts[3 * z + 1]
    final[2] = parts[3 * pair + 2]
    final[3] = parts[3 * pair + 5]

    def hop(t, part, c, buf, copy, receives, sends):
        low, high = span(t, part)
        rows = pl.ds(pl.multiple_of(c * chunk, 16), chunk)
        column = 3 * t + part

        @pl.when(receives)
        def _():
            copy(column, c).wait_recv()
            arrived = buf[column, rows, :].astype(F32)

            @pl.when(sends)
            def _():
                buf[column, rows, :] = (parts[column, rows, :] + arrived).astype(BF16)
                copy(column, c).start()

            @pl.when(jnp.logical_and(low <= z, z <= high))
            def _():
                slot = part if part < 2 else 2 + t % 2
                final[slot, rows, :] += arrived

    def hop_up(t, part, c):
        high = span(t, part)[1]
        hop(t, part, c, up, chain_up, jnp.logical_and(z > 0, z <= high), z < high)

    def hop_down(t, part, c):
        low = span(t, part)[0]
        hop(t, part, c, down, chain_down, jnp.logical_and(z < tensor_n - 1, z >= low), z > low)

    rounds = tensor_n * chunks
    lag = jnp.abs(tensor_n - 1 - 2 * z)
    up_lag = jnp.where(2 * z < tensor_n, 0, lag)
    down_lag = lag - up_lag

    def turn(n):
        def one(n, hop_one, mirror):
            slab_of = jnp.clip(n, 0, rounds - 1) // chunks
            t = tensor_n - 1 - slab_of if mirror else slab_of
            late = n >= rounds
            c = jnp.where(late, n - rounds, n % chunks)
            t = jnp.where(late, tensor_n - 2 if mirror else 1, t)

            @pl.when(jnp.logical_and(n >= 0, n < rounds + chunks))
            def _():
                @pl.when(jnp.logical_or(late, slab_of != 1))
                def _():
                    hop_one(t, 0, c)
                    hop_one(t, 1, c)

                @pl.when(jnp.logical_not(late))
                def _():
                    hop_one(t, 2, c)

        one(n - up_lag, hop_up, False)
        one(n - down_lag, hop_down, True)

    def prepared(raw, gains, rows):
        scaled = raw * lax.rsqrt(jnp.mean(raw * raw, axis=1, keepdims=True) + 1e-06) * gains
        return scaled * cos_ref[rows, :] + pltpu.roll(scaled, head // 2, 1) * sin_ref[rows, :]

    key_gain = key_gain_ref[pl.ds(z // 2, 1), :]
    live = len_ref[0]

    def attend(c):
        rows = pl.ds(c * chunk, chunk)
        seen = (c + 1) * chunk
        keys[rows, :] = prepared(final[2, rows, :], key_gain, rows).astype(BF16)
        values[rows, :] = final[3, rows, :].astype(BF16)
        row_pos = lax.broadcasted_iota(jnp.int32, (chunk, seen), 0) + c * chunk
        col_pos = lax.broadcasted_iota(jnp.int32, (chunk, seen), 1)
        allowed = jnp.logical_and(col_pos <= row_pos, col_pos < live)
        for j in range(2):
            raw = final[j, rows, :]
            query = (prepared(raw, query_gain_ref[j : j + 1, :], rows) * head ** (-0.5)).astype(BF16)
            scores = lax.dot_general(query, keys[:seen, :], (((1,), (1,)), ((), ())), preferred_element_type=F32)
            scores = jnp.where(allowed, scores, -1e30)
            exps = jnp.exp(scores - jnp.max(scores, axis=1, keepdims=True))
            probs = (exps / jnp.sum(exps, axis=1, keepdims=True)).astype(BF16)
            out_ref[rows, j * head : (j + 1) * head] = jnp.dot(
                probs, values[:seen, :], preferred_element_type=F32
            ).astype(BF16)

    at_end = jnp.logical_or(z == 0, z == tensor_n - 1)
    next_to = jnp.logical_or(z == 1, z == tensor_n - 2)

    def stop(c):
        end = rounds - chunks + c + 1 + lag
        beside = rounds + jnp.maximum(c + 1, lag)
        return jnp.where(at_end, end, jnp.where(next_to, beside, rounds + chunks + lag))

    for c in range(chunks):
        @pl.loop(0 if c == 0 else stop(c - 1), stop(c))
        def _(n):
            turn(n)

        attend(c)

    for i in range(1, plane_n):
        exchange(plane_sum, me, plane_peer(i)[1], plane_send.at[i], plane_recv).wait_send()
    for i in range(1, tensor_n):
        dev = line_peer(i)[1]
        exchange(line_sum, z, dev, line_send.at[i], line_recv).wait_send()
        exchange(row_sum, z, dev, row_send.at[i], row_recv).wait_send()

    for part in range(3):
        for h in range(1, chip_n):
            to_hub(h, part).wait_send()

        @pl.when(z != owner)
        def _():
            to_hub(0, part).wait_send()

    @pl.loop(0, tensor_n)
    def _(t):
        for r in range(hubs):
            for h in range(chip_n):
                for part in range(3):
                    forwards(r, h, t, part, wait_send)

    @pl.loop(0, tensor_n)
    def _(t):
        for part in range(3):
            low, high = span(t, part)

            @pl.loop(0, chunks)
            def _(c):
                @pl.when(z < high)
                def _():
                    chain_up(3 * t + part, c).wait_send()

                @pl.when(z > low)
                def _():
                    chain_down(3 * t + part, c).wait_send()


def shards(sizes, activations, norm_gain, master_weight, grad, moment, variance, query_gain, key_gain, prompt_len):
    group_n, dp_n, tensor_n = sizes
    plane_n = group_n * dp_n
    hubs = plane_n // tensor_n
    width = norm_gain.shape[0]
    length, feat = activations.shape
    slab_rows, _, slots, head = master_weight.shape
    pair = 2 * head
    chip_n = group_n // 2
    columns = 3 * tensor_n
    chunk = 256 if length % 256 == 0 else length
    chunks = length // chunk
    cosine, sine = rope_tables(length, head)

    def flat(array):
        return array.reshape(slab_rows * slots, head)

    hbm = pl.BlockSpec(memory_space=pl.ANY)
    vmem = pl.BlockSpec(memory_space=pltpu.VMEM)
    dma = pltpu.SemaphoreType.DMA
    return pl.pallas_call(
        functools.partial(kernel, (group_n, dp_n, tensor_n, width)),
        out_shape=jax.ShapeDtypeStruct((length, pair), BF16),
        in_specs=[hbm, vmem, hbm, hbm, hbm, hbm, vmem, vmem, vmem, vmem, pl.BlockSpec(memory_space=pltpu.SMEM)],
        out_specs=vmem,
        scratch_shapes=[
            pltpu.VMEM((length, feat), BF16),
            pltpu.VMEM((length, feat), BF16),
            pltpu.VMEM((slab_rows * slots, head), F32),
            pltpu.VMEM((slots, slab_rows, head), BF16),
            pltpu.VMEM((slab_rows * slots, head), F32),
            pltpu.VMEM((slab_rows * slots, head), F32),
            pltpu.VMEM((slots, slab_rows, head), BF16),
            pltpu.VMEM((columns, feat, head), BF16),
            pltpu.VMEM((columns, length, head), F32),
            pltpu.VMEM((columns, length, head), BF16),
            pltpu.VMEM((columns, length, head), BF16),
            pltpu.VMEM((4, length, head), F32),
            pltpu.VMEM((length, head), BF16),
            pltpu.VMEM((length, head), BF16),
            pltpu.VMEM((plane_n, 8, head), F32),
            pltpu.VMEM((tensor_n, 8, head), F32),
            pltpu.VMEM((tensor_n, 8, length), F32),
            dma((5,)),
            dma((plane_n,)),
            dma((plane_n,)),
            dma((tensor_n,)),
            dma((tensor_n,)),
            dma((tensor_n,)),
            dma((tensor_n,)),
            dma((chip_n, 3)),
            dma((hubs * chip_n, tensor_n, 3)),
            dma((hubs * chip_n, tensor_n, 3, chip_n + dp_n - 1)),
            dma((columns, chunks)),
            dma((columns, chunks)),
            dma((columns, chunks)),
            dma((columns, chunks)),
        ],
        compiler_params=pltpu.CompilerParams(
            collective_id=0, has_side_effects=True, vmem_limit_bytes=60 * 1024 * 1024
        ),
        name="step_and_prefill",
    )(
        activations,
        norm_gain.reshape(tensor_n, 1, feat),
        flat(master_weight),
        jnp.transpose(grad.reshape(slab_rows, slots, head), (1, 0, 2)),
        flat(moment),
        flat(variance),
        query_gain,
        key_gain,
        cosine,
        sine,
        prompt_len,
    )


def solution(mesh):
    in_specs = (
        P(("group", "dp"), "tensor"),
        P(),
        P(("group", "dp"), "tensor", None, None),
        P(("group", "dp"), "tensor", None, None),
        P(("group", "dp"), "tensor", None, None),
        P(("group", "dp"), "tensor", None, None),
        P("tensor", None),
        P(),
        P(("group", "dp")),
    )
    out_specs = P(("group", "dp"), "tensor")
    sizes = tuple(mesh.shape[axis] for axis in ("group", "dp", "tensor"))
    return jax.shard_map(
        functools.partial(shards, sizes), mesh=mesh, in_specs=in_specs, out_specs=out_specs, check_vma=False
    )
```

```python
import functools

import jax
import jax.numpy as jnp
import numpy as np
from jax import lax
from jax.experimental import pallas as pl
from jax.experimental.pallas import tpu as pltpu
from jax.sharding import PartitionSpec as P

STEP_SCALE = 0.5
BETA_ONE = 0.9
BETA_TWO = 0.95
ROPE_BASE = 500000.0
MESH = pl.DeviceIdType.MESH
BF16 = jnp.bfloat16
F32 = jnp.float32


def rope_tables(length, head_size):
    positions = np.arange(length, dtype=np.float32)
    exponent = np.arange(head_size // 2, dtype=np.float32) * np.float32(2.0) / np.float32(head_size)
    inverse = np.power(np.float32(ROPE_BASE), -exponent).astype(np.float32)
    angles = (positions[:, None] * inverse[None, :]).astype(np.float32)
    cosine, sine = np.cos(angles), np.sin(angles)
    return (
        np.concatenate([cosine, cosine], axis=1).astype(np.float32),
        np.concatenate([-sine, sine], axis=1).astype(np.float32),
    )


def kernel(
    sizes,
    act_hbm, gain_ref, master_hbm, grad_hbm, moment_hbm, variance_hbm, query_gain_ref, key_gain_ref,
    cos_ref, sin_ref, len_ref,
    out_ref,
    act, normed, master, grad, moment, variance, own, weights, parts, up, down, final, keys, values,
    plane_sum, line_sum, row_sum,
    in_sem, plane_send, plane_recv, line_send, line_recv, row_send, row_recv,
    hub_send, w_recv, w_send, up_send, up_recv, down_send, down_recv,
):
    group_n, dp_n, tensor_n, width = sizes
    plane_n = group_n * dp_n
    chip_n = group_n // 2
    hubs = plane_n // tensor_n
    length, feat = act.shape
    slab_rows = grad.shape[1]
    head = 128
    chunk = 256 if length % 256 == 0 else length
    chunks = length // chunk

    g = lax.axis_index("group")
    d = lax.axis_index("dp")
    z = lax.axis_index("tensor")
    me = g * dp_n + d
    x, core = g // 2, g % 2

    def plane_peer(i):
        p = (me + i) % plane_n
        return p, (p // dp_n, p % dp_n, z)

    def line_peer(i):
        t = (z + i) % tensor_n
        return t, (g, d, t)

    loads = [
        pltpu.make_async_copy(src, dst, in_sem.at[i])
        for i, (src, dst) in enumerate(
            [(grad_hbm, grad), (act_hbm, act), (moment_hbm, moment), (variance_hbm, variance), (master_hbm, master)]
        )
    ]
    for load in loads:
        load.start()

    barrier = pltpu.get_barrier_semaphore()
    for i in range(1, plane_n):
        pl.semaphore_signal(barrier, inc=1, device_id=plane_peer(i)[1], device_id_type=MESH)
    for i in range(1, tensor_n):
        pl.semaphore_signal(barrier, inc=1, device_id=line_peer(i)[1], device_id_type=MESH)

    loads[0].wait()
    tile = jnp.zeros((8, head), F32)
    for s in range(3):
        piece = grad[s].astype(F32)
        tile += jnp.sum((piece * piece).reshape(slab_rows // 8, 8, head), axis=0)
    plane_sum[me] = tile
    pl.semaphore_wait(barrier, plane_n + tensor_n - 2)

    def exchange(buf, slot, dev, ssem, rsem):
        return pltpu.make_async_remote_copy(
            src_ref=buf.at[slot], dst_ref=buf.at[slot], send_sem=ssem, recv_sem=rsem.at[slot],
            device_id=dev, device_id_type=MESH,
        )

    for i in range(1, plane_n):
        exchange(plane_sum, me, plane_peer(i)[1], plane_send.at[i], plane_recv).start()

    loads[1].wait()
    for c in range(chunks):
        rows = pl.ds(c * chunk, chunk)
        wide = act[rows, :].astype(F32)
        column = jnp.sum(wide * wide, axis=1, keepdims=True)
        row_sum[z, :, rows] = jnp.broadcast_to(column, (chunk, head)).T[:8]
    for i in range(1, tensor_n):
        exchange(row_sum, z, line_peer(i)[1], row_send.at[i], row_recv).start()

    total = plane_sum[me]
    for i in range(1, plane_n):
        p, dev = plane_peer(i)
        exchange(plane_sum, p, dev, plane_send.at[i], plane_recv).wait_recv()
        total += plane_sum[p]
    line_sum[z] = total
    for i in range(1, tensor_n):
        exchange(line_sum, z, line_peer(i)[1], line_send.at[i], line_recv).start()
    square = row_sum[z]
    for i in range(1, tensor_n):
        t, dev = line_peer(i)
        exchange(row_sum, t, dev, row_send.at[i], row_recv).wait_recv()
        square += row_sum[t]
    scale_row = lax.rsqrt(square[:1] * (1.0 / width) + 1e-06)
    for c in range(chunks):
        rows = pl.ds(c * chunk, chunk)
        scale = jnp.broadcast_to(scale_row[:, c * chunk : (c + 1) * chunk], (head, chunk)).T[:, :1]
        normed[rows, :] = (act[rows, :].astype(F32) * scale * gain_ref[z]).astype(BF16)

    for load in loads[2:]:
        load.wait()
    for i in range(1, tensor_n):
        t, dev = line_peer(i)
        exchange(line_sum, t, dev, line_send.at[i], line_recv).wait_recv()
        total += line_sum[t]
    sumsq = jnp.sum(jnp.sum(total, axis=0, keepdims=True), axis=1, keepdims=True)
    clip = 1.0 / jnp.sqrt(sumsq + 1e-12)

    step_size = STEP_SCALE * width ** (-0.5)

    def updated(s):
        clipped = grad[s].astype(F32) * clip
        rows = pl.ds(s, slab_rows, stride=3)
        moment_new = BETA_ONE * moment[rows, :] + (1.0 - BETA_ONE) * clipped
        variance_new = BETA_TWO * variance[rows, :] + (1.0 - BETA_TWO) * clipped * clipped
        return (master[rows, :] - step_size * moment_new / (jnp.sqrt(variance_new) + 1e-08)).astype(BF16)

    def w_slot(r, t, part):
        rows = pl.ds(pl.multiple_of(r * slab_rows, 16), slab_rows)
        return weights.at[3 * t + part, rows, :]

    owner, my_r = me // hubs, me % hubs

    def to_hub(part):
        return pltpu.make_async_remote_copy(
            src_ref=own.at[part], dst_ref=w_slot(my_r, z, part), send_sem=hub_send.at[part],
            recv_sem=w_recv.at[my_r, z, part], device_id=(g, d, owner), device_id_type=MESH,
        )

    def place(part):
        @pl.when(z == owner)
        def _():
            w_slot(my_r, z, part)[...] = own[part]

        @pl.when(z != owner)
        def _():
            to_hub(part).start()

    for part in (2, 0, 1):
        own[part] = updated(part)
        place(part)

    def forward(r, t, part, slot, dev):
        return pltpu.make_async_remote_copy(
            src_ref=w_slot(r, t, part), dst_ref=w_slot(r, t, part), send_sem=w_send.at[r, t, part, slot],
            recv_sem=w_recv.at[r, t, part], device_id=dev, device_id_type=MESH,
        )

    def forwards(r, t, part, act_on):
        hub = z * hubs + r
        hub_g, hub_d = hub // dp_n, hub % dp_n
        same_core = core == hub_g % 2
        at_hub = hub == me

        @pl.when(at_hub)
        def _():
            for i in range(1, chip_n):
                act_on(forward(r, t, part, i - 1, (((x + i) % chip_n) * 2 + core, d, z)))

        @pl.when(jnp.logical_and(same_core, d == hub_d))
        def _():
            for i in range(1, dp_n):
                act_on(forward(r, t, part, chip_n - 2 + i, (g, (d + i) % dp_n, z)))

        @pl.when(same_core)
        def _():
            act_on(forward(r, t, part, chip_n + dp_n - 2, (x * 2 + 1 - core, d, z)))

    def start(copy):
        copy.start()

    def wait_send(copy):
        copy.wait_send()

    def chain(buf, column, c, dev_z, ssem, rsem):
        rows = pl.ds(pl.multiple_of(c * chunk, 16), chunk)
        return pltpu.make_async_remote_copy(
            src_ref=buf.at[column, rows, :], dst_ref=buf.at[column, rows, :], send_sem=ssem.at[column, c],
            recv_sem=rsem.at[column, c], device_id=(g, d, dev_z), device_id_type=MESH,
        )

    def chain_up(column, c):
        return chain(up, column, c, jnp.minimum(z + 1, tensor_n - 1), up_send, up_recv)

    def chain_down(column, c):
        return chain(down, column, c, jnp.maximum(z - 1, 0), down_send, down_recv)

    def span(t, part):
        first = t if part < 2 else 2 * (t // 2)
        return first, first if part < 2 else first + 1

    def multiply(t, todo):
        @pl.loop(0, chunks)
        def _(c):
            rows = pl.ds(pl.multiple_of(c * chunk, 16), chunk)
            some = jnp.concatenate([weights[3 * t + part] for part in todo], axis=1)
            product = jnp.dot(normed[rows, :], some, preferred_element_type=F32)
            for i, part in enumerate(todo):
                parts[3 * t + part, rows, :] = product[:, i * head : (i + 1) * head]

            def begin(buf, copy, next_to):
                for part in todo:
                    buf[3 * t + part, rows, :] = parts[3 * t + part, rows, :].astype(BF16)
                    if part == 2:
                        copy(3 * t + part, c).start()
                    else:
                        @pl.when(jnp.logical_and(t != z, t != next_to))
                        def _():
                            copy(3 * t + part, c).start()

            @pl.when(z == 0)
            def _():
                begin(up, chain_up, 1)

            @pl.when(z == tensor_n - 1)
            def _():
                begin(down, chain_down, tensor_n - 2)

    def slab(j):
        room = jnp.minimum(z, tensor_n - 1 - z)
        near = z + ((j + 1) // 2) * (2 * (j % 2) - 1)
        far = jnp.where(z < tensor_n - 1 - z, j, tensor_n - 1 - j)
        return jnp.where(j <= 2 * room, near, far)

    def pass_on(t, i, todo):
        r = (d + i) % hubs
        for part in todo:
            @pl.when(jnp.logical_not(jnp.logical_and(z * hubs + r == me, t == z)))
            def _():
                forward(r, t, part, 0, (g, d, z)).wait_recv()

            forwards(r, t, part, start)

    pass_on(slab(0), 0, (2, 0, 1))

    @pl.loop(0, tensor_n)
    def _(j):
        t = slab(j)
        for i in range(1, hubs):
            pass_on(t, i, (2,))
        multiply(t, (2,))

        @pl.when(j + 1 < tensor_n)
        def _():
            pass_on(slab(jnp.minimum(j + 1, tensor_n - 1)), 0, (2, 0, 1))

        for i in range(1, hubs):
            pass_on(t, i, (0, 1))
        multiply(t, (0, 1))

    @pl.when(z == 0)
    def _():
        for c in range(chunks):
            for part in range(2):
                chain_up(3 + part, c).start()

    @pl.when(z == tensor_n - 1)
    def _():
        for c in range(chunks):
            for part in range(2):
                chain_down(3 * (tensor_n - 2) + part, c).start()

    pair = 2 * (z // 2)
    final[0] = parts[3 * z]
    final[1] = parts[3 * z + 1]
    final[2] = parts[3 * pair + 2]
    final[3] = parts[3 * pair + 5]

    def hop(t, part, c, buf, copy, receives, sends):
        low, high = span(t, part)
        rows = pl.ds(pl.multiple_of(c * chunk, 16), chunk)
        column = 3 * t + part

        @pl.when(receives)
        def _():
            copy(column, c).wait_recv()
            arrived = buf[column, rows, :].astype(F32)

            @pl.when(sends)
            def _():
                buf[column, rows, :] = (parts[column, rows, :] + arrived).astype(BF16)
                copy(column, c).start()

            @pl.when(jnp.logical_and(low <= z, z <= high))
            def _():
                slot = part if part < 2 else 2 + t % 2
                final[slot, rows, :] += arrived

    def hop_up(t, part, c):
        high = span(t, part)[1]
        hop(t, part, c, up, chain_up, jnp.logical_and(z > 0, z <= high), z < high)

    def hop_down(t, part, c):
        low = span(t, part)[0]
        hop(t, part, c, down, chain_down, jnp.logical_and(z < tensor_n - 1, z >= low), z > low)

    per_slab = chunks + 1
    rounds = tensor_n * per_slab
    lag = jnp.abs(tensor_n - 1 - 2 * z)
    up_lag = jnp.where(2 * z < tensor_n, 0, lag)
    down_lag = lag - up_lag

    def turn(n):
        def one(n, hop_one, mirror):
            slab_of = jnp.clip(n, 0, rounds - 1) // per_slab
            t = tensor_n - 1 - slab_of if mirror else slab_of
            late = n >= rounds
            place = jnp.clip(n, 0, rounds - 1) % per_slab
            c = jnp.where(late, n - rounds, jnp.maximum(place - 1, 0))
            t = jnp.where(late, tensor_n - 2 if mirror else 1, t)
            whole = jnp.logical_and(jnp.logical_not(late), place == 0)

            @pl.when(jnp.logical_and(n >= 0, n < rounds + chunks))
            def _():
                @pl.when(whole)
                def _():
                    for i in range(chunks):
                        hop_one(t, 2, i)

                @pl.when(jnp.logical_and(jnp.logical_not(whole), jnp.logical_or(late, slab_of != 1)))
                def _():
                    hop_one(t, 0, c)
                    hop_one(t, 1, c)

        one(n - up_lag, hop_up, False)
        one(n - down_lag, hop_down, True)

    def prepared(raw, gains, rows):
        scaled = raw * lax.rsqrt(jnp.mean(raw * raw, axis=1, keepdims=True) + 1e-06) * gains
        return scaled * cos_ref[rows, :] + pltpu.roll(scaled, head // 2, 1) * sin_ref[rows, :]

    key_gain = key_gain_ref[pl.ds(z // 2, 1), :]
    live = len_ref[0]

    def attend(c):
        rows = pl.ds(c * chunk, chunk)
        seen = (c + 1) * chunk
        keys[rows, :] = prepared(final[2, rows, :], key_gain, rows).astype(BF16)
        values[rows, :] = final[3, rows, :].astype(BF16)
        row_pos = lax.broadcasted_iota(jnp.int32, (chunk, seen), 0) + c * chunk
        col_pos = lax.broadcasted_iota(jnp.int32, (chunk, seen), 1)
        allowed = jnp.logical_and(col_pos <= row_pos, col_pos < live)
        for j in range(2):
            raw = final[j, rows, :]
            query = (prepared(raw, query_gain_ref[j : j + 1, :], rows) * head ** (-0.5)).astype(BF16)
            scores = lax.dot_general(query, keys[:seen, :], (((1,), (1,)), ((), ())), preferred_element_type=F32)
            scores = jnp.where(allowed, scores, -1e30)
            exps = jnp.exp(scores - jnp.max(scores, axis=1, keepdims=True))
            probs = (exps / jnp.sum(exps, axis=1, keepdims=True)).astype(BF16)
            out_ref[rows, j * head : (j + 1) * head] = jnp.dot(
                probs, values[:seen, :], preferred_element_type=F32
            ).astype(BF16)

    at_end = jnp.logical_or(z == 0, z == tensor_n - 1)
    next_to = jnp.logical_or(z == 1, z == tensor_n - 2)

    def stop(c):
        end = rounds - chunks + c + 1 + lag
        beside = rounds + jnp.maximum(c + 1, lag)
        return jnp.where(at_end, end, jnp.where(next_to, beside, rounds + chunks + lag))

    for c in range(chunks):
        @pl.loop(0 if c == 0 else stop(c - 1), stop(c))
        def _(n):
            turn(n)

        attend(c)

    for i in range(1, plane_n):
        exchange(plane_sum, me, plane_peer(i)[1], plane_send.at[i], plane_recv).wait_send()
    for i in range(1, tensor_n):
        dev = line_peer(i)[1]
        exchange(line_sum, z, dev, line_send.at[i], line_recv).wait_send()
        exchange(row_sum, z, dev, row_send.at[i], row_recv).wait_send()

    @pl.when(z != owner)
    def _():
        for part in range(3):
            to_hub(part).wait_send()

    @pl.loop(0, tensor_n)
    def _(t):
        for r in range(hubs):
            for part in range(3):
                forwards(r, t, part, wait_send)

    @pl.loop(0, tensor_n)
    def _(t):
        for part in range(3):
            low, high = span(t, part)

            @pl.loop(0, chunks)
            def _(c):
                @pl.when(z < high)
                def _():
                    chain_up(3 * t + part, c).wait_send()

                @pl.when(z > low)
                def _():
                    chain_down(3 * t + part, c).wait_send()


def shards(sizes, activations, norm_gain, master_weight, grad, moment, variance, query_gain, key_gain, prompt_len):
    group_n, dp_n, tensor_n = sizes
    plane_n = group_n * dp_n
    hubs = plane_n // tensor_n
    width = norm_gain.shape[0]
    length, feat = activations.shape
    slab_rows, _, slots, head = master_weight.shape
    pair = 2 * head
    columns = 3 * tensor_n
    chunk = 256 if length % 256 == 0 else length
    chunks = length // chunk
    cosine, sine = rope_tables(length, head)

    def flat(array):
        return array.reshape(slab_rows * slots, head)

    hbm = pl.BlockSpec(memory_space=pl.ANY)
    vmem = pl.BlockSpec(memory_space=pltpu.VMEM)
    dma = pltpu.SemaphoreType.DMA
    return pl.pallas_call(
        functools.partial(kernel, (group_n, dp_n, tensor_n, width)),
        out_shape=jax.ShapeDtypeStruct((length, pair), BF16),
        in_specs=[hbm, vmem, hbm, hbm, hbm, hbm, vmem, vmem, vmem, vmem, pl.BlockSpec(memory_space=pltpu.SMEM)],
        out_specs=vmem,
        scratch_shapes=[
            pltpu.VMEM((length, feat), BF16),
            pltpu.VMEM((length, feat), BF16),
            pltpu.VMEM((slab_rows * slots, head), F32),
            pltpu.VMEM((slots, slab_rows, head), BF16),
            pltpu.VMEM((slab_rows * slots, head), F32),
            pltpu.VMEM((slab_rows * slots, head), F32),
            pltpu.VMEM((slots, slab_rows, head), BF16),
            pltpu.VMEM((columns, feat, head), BF16),
            pltpu.VMEM((columns, length, head), F32),
            pltpu.VMEM((columns, length, head), BF16),
            pltpu.VMEM((columns, length, head), BF16),
            pltpu.VMEM((4, length, head), F32),
            pltpu.VMEM((length, head), BF16),
            pltpu.VMEM((length, head), BF16),
            pltpu.VMEM((plane_n, 8, head), F32),
            pltpu.VMEM((tensor_n, 8, head), F32),
            pltpu.VMEM((tensor_n, 8, length), F32),
            dma((5,)),
            dma((plane_n,)),
            dma((plane_n,)),
            dma((tensor_n,)),
            dma((tensor_n,)),
            dma((tensor_n,)),
            dma((tensor_n,)),
            dma((3,)),
            dma((hubs, tensor_n, 3)),
            dma((hubs, tensor_n, 3, group_n // 2 + dp_n - 1)),
            dma((columns, chunks)),
            dma((columns, chunks)),
            dma((columns, chunks)),
            dma((columns, chunks)),
        ],
        compiler_params=pltpu.CompilerParams(
            collective_id=0, has_side_effects=True, vmem_limit_bytes=60 * 1024 * 1024
        ),
        name="step_and_prefill",
    )(
        activations,
        norm_gain.reshape(tensor_n, 1, feat),
        flat(master_weight),
        jnp.transpose(grad.reshape(slab_rows, slots, head), (1, 0, 2)),
        flat(moment),
        flat(variance),
        query_gain,
        key_gain,
        cosine,
        sine,
        prompt_len,
    )


def solution(mesh):
    in_specs = (
        P(("group", "dp"), "tensor"),
        P(),
        P(("group", "dp"), "tensor", None, None),
        P(("group", "dp"), "tensor", None, None),
        P(("group", "dp"), "tensor", None, None),
        P(("group", "dp"), "tensor", None, None),
        P("tensor", None),
        P(),
        P(("group", "dp")),
    )
    out_specs = P(("group", "dp"), "tensor")
    sizes = tuple(mesh.shape[axis] for axis in ("group", "dp", "tensor"))
    return jax.shard_map(
        functools.partial(shards, sizes), mesh=mesh, in_specs=in_specs, out_specs=out_specs, check_vma=False
    )
```

```python
import functools

import jax
import jax.numpy as jnp
import numpy as np
from jax import lax
from jax.experimental import pallas as pl
from jax.experimental.pallas import tpu as pltpu
from jax.sharding import PartitionSpec as P

STEP_SCALE = 0.5
BETA_ONE = 0.9
BETA_TWO = 0.95
ROPE_BASE = 500000.0
MESH = pl.DeviceIdType.MESH
BF16 = jnp.bfloat16
F32 = jnp.float32


def rope_tables(length, head_size):
    positions = np.arange(length, dtype=np.float32)
    exponent = np.arange(head_size // 2, dtype=np.float32) * np.float32(2.0) / np.float32(head_size)
    inverse = np.power(np.float32(ROPE_BASE), -exponent).astype(np.float32)
    angles = (positions[:, None] * inverse[None, :]).astype(np.float32)
    cosine, sine = np.cos(angles), np.sin(angles)
    return (
        np.concatenate([cosine, cosine], axis=1).astype(np.float32),
        np.concatenate([-sine, sine], axis=1).astype(np.float32),
    )


def kernel(
    sizes,
    act_hbm, gain_ref, master_hbm, grad_hbm, moment_hbm, variance_hbm, query_gain_ref, key_gain_ref,
    cos_ref, sin_ref, len_ref,
    out_ref,
    act, normed, master, grad, moment, variance, own, weights, parts, up, down, final, keys, values,
    plane_sum, line_sum, row_sum,
    in_sem, plane_send, plane_recv, line_send, line_recv, row_send, row_recv,
    hub_send, w_recv, w_send, up_send, up_recv, down_send, down_recv,
):
    group_n, dp_n, tensor_n, width = sizes
    plane_n = group_n * dp_n
    chip_n = group_n // 2
    hubs = plane_n // tensor_n
    length, feat = act.shape
    slab_rows = grad.shape[1]
    head = 128
    chunk = 256 if length % 256 == 0 else length
    chunks = length // chunk

    g = lax.axis_index("group")
    d = lax.axis_index("dp")
    z = lax.axis_index("tensor")
    me = g * dp_n + d
    x, core = g // 2, g % 2

    def plane_peer(i):
        p = (me + i) % plane_n
        return p, (p // dp_n, p % dp_n, z)

    def line_peer(i):
        t = (z + i) % tensor_n
        return t, (g, d, t)

    loads = [
        pltpu.make_async_copy(src, dst, in_sem.at[i])
        for i, (src, dst) in enumerate(
            [(grad_hbm, grad), (act_hbm, act), (moment_hbm, moment), (variance_hbm, variance), (master_hbm, master)]
        )
    ]
    for load in loads:
        load.start()

    barrier = pltpu.get_barrier_semaphore()
    for i in range(1, plane_n):
        pl.semaphore_signal(barrier, inc=1, device_id=plane_peer(i)[1], device_id_type=MESH)
    for i in range(1, tensor_n):
        pl.semaphore_signal(barrier, inc=1, device_id=line_peer(i)[1], device_id_type=MESH)

    loads[0].wait()
    tile = jnp.zeros((8, head), F32)
    for s in range(3):
        piece = grad[s].astype(F32)
        tile += jnp.sum((piece * piece).reshape(slab_rows // 8, 8, head), axis=0)
    plane_sum[me] = tile
    pl.semaphore_wait(barrier, plane_n + tensor_n - 2)

    def exchange(buf, slot, dev, ssem, rsem):
        return pltpu.make_async_remote_copy(
            src_ref=buf.at[slot], dst_ref=buf.at[slot], send_sem=ssem, recv_sem=rsem.at[slot],
            device_id=dev, device_id_type=MESH,
        )

    for i in range(1, plane_n):
        exchange(plane_sum, me, plane_peer(i)[1], plane_send.at[i], plane_recv).start()

    loads[1].wait()
    for c in range(chunks):
        rows = pl.ds(c * chunk, chunk)
        wide = act[rows, :].astype(F32)
        column = jnp.sum(wide * wide, axis=1, keepdims=True)
        row_sum[z, :, rows] = jnp.broadcast_to(column, (chunk, head)).T[:8]
    for i in range(1, tensor_n):
        exchange(row_sum, z, line_peer(i)[1], row_send.at[i], row_recv).start()

    total = plane_sum[me]
    for i in range(1, plane_n):
        p, dev = plane_peer(i)
        exchange(plane_sum, p, dev, plane_send.at[i], plane_recv).wait_recv()
        total += plane_sum[p]
    line_sum[z] = total
    for i in range(1, tensor_n):
        exchange(line_sum, z, line_peer(i)[1], line_send.at[i], line_recv).start()
    square = row_sum[z]
    for i in range(1, tensor_n):
        t, dev = line_peer(i)
        exchange(row_sum, t, dev, row_send.at[i], row_recv).wait_recv()
        square += row_sum[t]
    scale_row = lax.rsqrt(square[:1] * (1.0 / width) + 1e-06)
    for c in range(chunks):
        rows = pl.ds(c * chunk, chunk)
        scale = jnp.broadcast_to(scale_row[:, c * chunk : (c + 1) * chunk], (head, chunk)).T[:, :1]
        normed[rows, :] = (act[rows, :].astype(F32) * scale * gain_ref[z]).astype(BF16)

    for load in loads[2:]:
        load.wait()
    for i in range(1, tensor_n):
        t, dev = line_peer(i)
        exchange(line_sum, t, dev, line_send.at[i], line_recv).wait_recv()
        total += line_sum[t]
    sumsq = jnp.sum(jnp.sum(total, axis=0, keepdims=True), axis=1, keepdims=True)
    clip = 1.0 / jnp.sqrt(sumsq + 1e-12)

    step_size = STEP_SCALE * width ** (-0.5)

    def updated(s):
        clipped = grad[s].astype(F32) * clip
        rows = pl.ds(s, slab_rows, stride=3)
        moment_new = BETA_ONE * moment[rows, :] + (1.0 - BETA_ONE) * clipped
        variance_new = BETA_TWO * variance[rows, :] + (1.0 - BETA_TWO) * clipped * clipped
        return (master[rows, :] - step_size * moment_new / (jnp.sqrt(variance_new) + 1e-08)).astype(BF16)

    def w_slot(r, t, part):
        rows = pl.ds(pl.multiple_of(r * slab_rows, 16), slab_rows)
        return weights.at[3 * t + part, rows, :]

    owner, my_r = me // hubs, me % hubs

    def to_hub(part):
        return pltpu.make_async_remote_copy(
            src_ref=own.at[part], dst_ref=w_slot(my_r, z, part), send_sem=hub_send.at[part],
            recv_sem=w_recv.at[my_r, z, part], device_id=(g, d, owner), device_id_type=MESH,
        )

    def place(part):
        @pl.when(z == owner)
        def _():
            w_slot(my_r, z, part)[...] = own[part]

        @pl.when(z != owner)
        def _():
            to_hub(part).start()

    for part in range(3):
        own[part] = updated(part)
        place(part)

    def forward(r, t, part, slot, dev):
        return pltpu.make_async_remote_copy(
            src_ref=w_slot(r, t, part), dst_ref=w_slot(r, t, part), send_sem=w_send.at[r, t, part, slot],
            recv_sem=w_recv.at[r, t, part], device_id=dev, device_id_type=MESH,
        )

    def forwards(r, t, part, act_on):
        hub = z * hubs + r
        hub_g, hub_d = hub // dp_n, hub % dp_n
        same_core = core == hub_g % 2
        at_hub = hub == me

        @pl.when(at_hub)
        def _():
            for i in range(1, chip_n):
                act_on(forward(r, t, part, i - 1, (((x + i) % chip_n) * 2 + core, d, z)))

        @pl.when(jnp.logical_and(same_core, d == hub_d))
        def _():
            for i in range(1, dp_n):
                act_on(forward(r, t, part, chip_n - 2 + i, (g, (d + i) % dp_n, z)))

        @pl.when(same_core)
        def _():
            act_on(forward(r, t, part, chip_n + dp_n - 2, (x * 2 + 1 - core, d, z)))

    def start(copy):
        copy.start()

    def wait_send(copy):
        copy.wait_send()

    def chain(buf, column, c, dev_z, ssem, rsem):
        rows = pl.ds(pl.multiple_of(c * chunk, 16), chunk)
        return pltpu.make_async_remote_copy(
            src_ref=buf.at[column, rows, :], dst_ref=buf.at[column, rows, :], send_sem=ssem.at[column, c],
            recv_sem=rsem.at[column, c], device_id=(g, d, dev_z), device_id_type=MESH,
        )

    def chain_up(column, c):
        return chain(up, column, c, jnp.minimum(z + 1, tensor_n - 1), up_send, up_recv)

    def chain_down(column, c):
        return chain(down, column, c, jnp.maximum(z - 1, 0), down_send, down_recv)

    def span(t, part):
        first = t if part < 2 else 2 * (t // 2)
        return first, first if part < 2 else first + 1

    def multiply(t):
        @pl.loop(0, chunks)
        def _(c):
            rows = pl.ds(pl.multiple_of(c * chunk, 16), chunk)
            both = jnp.concatenate([weights[3 * t], weights[3 * t + 1]], axis=1)
            product = jnp.dot(normed[rows, :], both, preferred_element_type=F32)
            parts[3 * t, rows, :] = product[:, :head]
            parts[3 * t + 1, rows, :] = product[:, head:]
            parts[3 * t + 2, rows, :] = jnp.dot(normed[rows, :], weights[3 * t + 2], preferred_element_type=F32)

            def begin(buf, copy, next_to):
                for part in range(3):
                    buf[3 * t + part, rows, :] = parts[3 * t + part, rows, :].astype(BF16)
                    if part == 2:
                        copy(3 * t + part, c).start()
                    else:
                        @pl.when(jnp.logical_and(t != z, t != next_to))
                        def _():
                            copy(3 * t + part, c).start()

            @pl.when(z == 0)
            def _():
                begin(up, chain_up, 1)

            @pl.when(z == tensor_n - 1)
            def _():
                begin(down, chain_down, tensor_n - 2)

    def slab(j):
        room = jnp.minimum(z, tensor_n - 1 - z)
        near = z + ((j + 1) // 2) * (2 * (j % 2) - 1)
        far = jnp.where(z < tensor_n - 1 - z, j, tensor_n - 1 - j)
        return jnp.where(j <= 2 * room, near, far)

    def pass_on(t, i):
        r = (d + i) % hubs
        for part in range(3):
            @pl.when(jnp.logical_not(jnp.logical_and(z * hubs + r == me, t == z)))
            def _():
                forward(r, t, part, 0, (g, d, z)).wait_recv()

            forwards(r, t, part, start)

    pass_on(slab(0), 0)

    @pl.loop(0, tensor_n)
    def _(j):
        @pl.when(j + 1 < tensor_n)
        def _():
            pass_on(slab(jnp.minimum(j + 1, tensor_n - 1)), 0)

        t = slab(j)
        for i in range(1, hubs):
            pass_on(t, i)
        multiply(t)

    @pl.when(z == 0)
    def _():
        for c in range(chunks):
            for part in range(2):
                chain_up(3 + part, c).start()

    @pl.when(z == tensor_n - 1)
    def _():
        for c in range(chunks):
            for part in range(2):
                chain_down(3 * (tensor_n - 2) + part, c).start()

    pair = 2 * (z // 2)
    final[0] = parts[3 * z]
    final[1] = parts[3 * z + 1]
    final[2] = parts[3 * pair + 2]
    final[3] = parts[3 * pair + 5]

    def hop(t, part, c, buf, copy, receives, sends):
        low, high = span(t, part)
        rows = pl.ds(pl.multiple_of(c * chunk, 16), chunk)
        column = 3 * t + part

        @pl.when(receives)
        def _():
            copy(column, c).wait_recv()
            arrived = buf[column, rows, :].astype(F32)

            @pl.when(sends)
            def _():
                buf[column, rows, :] = (parts[column, rows, :] + arrived).astype(BF16)
                copy(column, c).start()

            @pl.when(jnp.logical_and(low <= z, z <= high))
            def _():
                slot = part if part < 2 else 2 + t % 2
                final[slot, rows, :] += arrived

    def hop_up(t, part, c):
        high = span(t, part)[1]
        hop(t, part, c, up, chain_up, jnp.logical_and(z > 0, z <= high), z < high)

    def hop_down(t, part, c):
        low = span(t, part)[0]
        hop(t, part, c, down, chain_down, jnp.logical_and(z < tensor_n - 1, z >= low), z > low)

    rounds = tensor_n * chunks
    lag = jnp.abs(tensor_n - 1 - 2 * z)
    up_lag = jnp.where(2 * z < tensor_n, 0, lag)
    down_lag = lag - up_lag

    def turn(n):
        def one(n, hop_one, mirror):
            slab_of = jnp.clip(n, 0, rounds - 1) // chunks
            t = tensor_n - 1 - slab_of if mirror else slab_of
            late = n >= rounds
            c = jnp.where(late, n - rounds, n % chunks)
            t = jnp.where(late, tensor_n - 2 if mirror else 1, t)

            @pl.when(jnp.logical_and(n >= 0, n < rounds + chunks))
            def _():
                @pl.when(jnp.logical_or(late, slab_of != 1))
                def _():
                    hop_one(t, 0, c)
                    hop_one(t, 1, c)

                @pl.when(jnp.logical_not(late))
                def _():
                    hop_one(t, 2, c)

        one(n - up_lag, hop_up, False)
        one(n - down_lag, hop_down, True)

    def prepared(raw, gains, rows):
        scaled = raw * lax.rsqrt(jnp.mean(raw * raw, axis=1, keepdims=True) + 1e-06) * gains
        return scaled * cos_ref[rows, :] + pltpu.roll(scaled, head // 2, 1) * sin_ref[rows, :]

    key_gain = key_gain_ref[pl.ds(z // 2, 1), :]
    live = len_ref[0]

    def attend(c):
        rows = pl.ds(c * chunk, chunk)
        seen = (c + 1) * chunk
        keys[rows, :] = prepared(final[2, rows, :], key_gain, rows).astype(BF16)
        values[rows, :] = final[3, rows, :].astype(BF16)
        row_pos = lax.broadcasted_iota(jnp.int32, (chunk, seen), 0) + c * chunk
        col_pos = lax.broadcasted_iota(jnp.int32, (chunk, seen), 1)
        allowed = jnp.logical_and(col_pos <= row_pos, col_pos < live)
        for j in range(2):
            raw = final[j, rows, :]
            query = (prepared(raw, query_gain_ref[j : j + 1, :], rows) * head ** (-0.5)).astype(BF16)
            scores = lax.dot_general(query, keys[:seen, :], (((1,), (1,)), ((), ())), preferred_element_type=F32)
            scores = jnp.where(allowed, scores, -1e30)
            exps = jnp.exp(scores - jnp.max(scores, axis=1, keepdims=True))
            probs = (exps / jnp.sum(exps, axis=1, keepdims=True)).astype(BF16)
            out_ref[rows, j * head : (j + 1) * head] = jnp.dot(
                probs, values[:seen, :], preferred_element_type=F32
            ).astype(BF16)

    at_end = jnp.logical_or(z == 0, z == tensor_n - 1)
    next_to = jnp.logical_or(z == 1, z == tensor_n - 2)

    def stop(c):
        end = rounds - chunks + c + 1 + lag
        beside = rounds + jnp.maximum(c + 1, lag)
        return jnp.where(at_end, end, jnp.where(next_to, beside, rounds + chunks + lag))

    for c in range(chunks):
        @pl.loop(0 if c == 0 else stop(c - 1), stop(c))
        def _(n):
            turn(n)

        attend(c)

    for i in range(1, plane_n):
        exchange(plane_sum, me, plane_peer(i)[1], plane_send.at[i], plane_recv).wait_send()
    for i in range(1, tensor_n):
        dev = line_peer(i)[1]
        exchange(line_sum, z, dev, line_send.at[i], line_recv).wait_send()
        exchange(row_sum, z, dev, row_send.at[i], row_recv).wait_send()

    @pl.when(z != owner)
    def _():
        for part in range(3):
            to_hub(part).wait_send()

    @pl.loop(0, tensor_n)
    def _(t):
        for r in range(hubs):
            for part in range(3):
                forwards(r, t, part, wait_send)

    @pl.loop(0, tensor_n)
    def _(t):
        for part in range(3):
            low, high = span(t, part)

            @pl.loop(0, chunks)
            def _(c):
                @pl.when(z < high)
                def _():
                    chain_up(3 * t + part, c).wait_send()

                @pl.when(z > low)
                def _():
                    chain_down(3 * t + part, c).wait_send()


def shards(sizes, activations, norm_gain, master_weight, grad, moment, variance, query_gain, key_gain, prompt_len):
    group_n, dp_n, tensor_n = sizes
    plane_n = group_n * dp_n
    hubs = plane_n // tensor_n
    width = norm_gain.shape[0]
    length, feat = activations.shape
    slab_rows, _, slots, head = master_weight.shape
    pair = 2 * head
    columns = 3 * tensor_n
    chunk = 256 if length % 256 == 0 else length
    chunks = length // chunk
    cosine, sine = rope_tables(length, head)

    def flat(array):
        return array.reshape(slab_rows * slots, head)

    hbm = pl.BlockSpec(memory_space=pl.ANY)
    vmem = pl.BlockSpec(memory_space=pltpu.VMEM)
    dma = pltpu.SemaphoreType.DMA
    return pl.pallas_call(
        functools.partial(kernel, (group_n, dp_n, tensor_n, width)),
        out_shape=jax.ShapeDtypeStruct((length, pair), BF16),
        in_specs=[hbm, vmem, hbm, hbm, hbm, hbm, vmem, vmem, vmem, vmem, pl.BlockSpec(memory_space=pltpu.SMEM)],
        out_specs=vmem,
        scratch_shapes=[
            pltpu.VMEM((length, feat), BF16),
            pltpu.VMEM((length, feat), BF16),
            pltpu.VMEM((slab_rows * slots, head), F32),
            pltpu.VMEM((slots, slab_rows, head), BF16),
            pltpu.VMEM((slab_rows * slots, head), F32),
            pltpu.VMEM((slab_rows * slots, head), F32),
            pltpu.VMEM((slots, slab_rows, head), BF16),
            pltpu.VMEM((columns, feat, head), BF16),
            pltpu.VMEM((columns, length, head), F32),
            pltpu.VMEM((columns, length, head), BF16),
            pltpu.VMEM((columns, length, head), BF16),
            pltpu.VMEM((4, length, head), F32),
            pltpu.VMEM((length, head), BF16),
            pltpu.VMEM((length, head), BF16),
            pltpu.VMEM((plane_n, 8, head), F32),
            pltpu.VMEM((tensor_n, 8, head), F32),
            pltpu.VMEM((tensor_n, 8, length), F32),
            dma((5,)),
            dma((plane_n,)),
            dma((plane_n,)),
            dma((tensor_n,)),
            dma((tensor_n,)),
            dma((tensor_n,)),
            dma((tensor_n,)),
            dma((3,)),
            dma((hubs, tensor_n, 3)),
            dma((hubs, tensor_n, 3, group_n // 2 + dp_n - 1)),
            dma((columns, chunks)),
            dma((columns, chunks)),
            dma((columns, chunks)),
            dma((columns, chunks)),
        ],
        compiler_params=pltpu.CompilerParams(
            collective_id=0, has_side_effects=True, vmem_limit_bytes=60 * 1024 * 1024
        ),
        name="step_and_prefill",
    )(
        activations,
        norm_gain.reshape(tensor_n, 1, feat),
        flat(master_weight),
        jnp.transpose(grad.reshape(slab_rows, slots, head), (1, 0, 2)),
        flat(moment),
        flat(variance),
        query_gain,
        key_gain,
        cosine,
        sine,
        prompt_len,
    )


def solution(mesh):
    in_specs = (
        P(("group", "dp"), "tensor"),
        P(),
        P(("group", "dp"), "tensor", None, None),
        P(("group", "dp"), "tensor", None, None),
        P(("group", "dp"), "tensor", None, None),
        P(("group", "dp"), "tensor", None, None),
        P("tensor", None),
        P(),
        P(("group", "dp")),
    )
    out_specs = P(("group", "dp"), "tensor")
    sizes = tuple(mesh.shape[axis] for axis in ("group", "dp", "tensor"))
    return jax.shard_map(
        functools.partial(shards, sizes), mesh=mesh, in_specs=in_specs, out_specs=out_specs, check_vma=False
    )
```
